32 devices in a mesh: groups: 2 (over x), branch: 16 (over z, y, core).
Axes of the slice: x: 2, y: 2, z: 4, core: 2. Of those that a mesh axis runs over, the one named last changes fastest.
Arguments:
- prompt_k: bfloat16 [32, 1024, 1024], P(('groups', 'branch')), parts along dimension 0, may hold values from -6 to 6
- prompt_v: bfloat16 [32, 1024, 1024], P(('groups', 'branch')), parts along dimension 0, may hold values from -6 to 6
- prompt_mask: int32 [32, 8], P(('groups', 'branch')), parts along dimension 0, may hold values from 0 to 1, as said below
- shared_kv: bfloat16 [64, 24, 2048], P(('groups', 'branch')), parts along dimension 0, may hold values from -6 to 6
- shared_len: int32 [64], P(('groups', 'branch')), parts along dimension 0, may hold values from 1 to 24, 400 in all
- send_pick: int32 [32, 16], P(('groups', 'branch')), parts along dimension 0, may hold values from -1 to 1, as said below
- unique_q: bfloat16 [512, 8192], P(('groups', 'branch')), parts along dimension 0, may hold values from -132 to 132
- unique_kv: bfloat16 [512, 2048], P(('groups', 'branch')), parts along dimension 0, may hold values from -6.5 to 6.5
- unique_owner: int32 [512, 1], P(('groups', 'branch')), parts along dimension 0, may hold values from 0 to 15; in each aligned block of 16 rows (0 to 15, 16 to 31, ...) at most 2 rows name the same one
Outputs:
- attended: bfloat16 [512, 8192], P(('groups', 'branch')), parts along dimension 0
The draws below stay inside these ranges and needn't reach their ends.
There are 2 independent parts, one for each index of `groups`. The reference program is written for one: setup_inputs(seed, part) draws one part's arguments, and reference() takes and returns one part's arrays. A program takes and returns all parts, laid end to end along the dimension named above; each array names one. Nothing has to cross between parts.
Inputs may be any that keep to these rules, and one draw needn't show every extreme that they name: `prompt_mask`: block 0 of every branch's prompt is visible. `send_pick`: entry [s, b] names which of owner s's 2 results branch b subscribes to, or -1 for none; every branch subscribes to exactly 12 results, at most one of each owner. `unique_owner`: among the rows of one source, no branch is named by more than 2 rows.
All inputs are finite; a program needn't handle non-finite values. No bound on the sum of `shared_len` on one device may be relied on, other than what follows from the above.
Results may differ from the reference program's by a relative error of at most 0.0027.
Values may be sent and summed in bfloat16 or wider, within the bound.
No kernel may reach another device: no remote copies, remote signals or barrier semaphores. Data moves between devices by JAX's collectives and lax.ppermute only.
A program may use at most 128 MiB of HBM per device.

```python
import math
import jax
import jax.numpy as jnp
import numpy as np
from jax import lax

QH = 64
KVH = 8
HD = 128
GRP = 8
QW = 8192
KVW = 1024
PLEN = 1024
PB = 128
PBLK = 8
RLEN = 24
RES_DEV = 2
NRES = 32
SUBS = 12
CAP = 2
UNQ_DEV = 16
ROWS = 256
N_BRANCH = 16


def draw_prompt_k(key, part):
    values = jnp.clip(jax.random.normal(jax.random.fold_in(key, 11), (N_BRANCH, PLEN, KVW), jnp.float32), -6.0, 6.0)
    return values.astype(jnp.bfloat16)


def draw_prompt_mask(key, part):
    levels = jax.random.randint(jax.random.fold_in(key, 19), (N_BRANCH, PBLK), 0, 4)
    visible = (levels > 0).astype(jnp.int32)
    return visible.at[:, 0].set(1)


def draw_send_pick(key, part):
    subkeys = jax.random.split(jax.random.fold_in(key, 23), N_BRANCH)
    ordering = jax.vmap(lambda single: jax.random.permutation(single, N_BRANCH))(subkeys)
    position = jnp.argsort(ordering, axis=1)
    which = jax.random.randint(jax.random.fold_in(key, 29), (N_BRANCH, N_BRANCH), 0, RES_DEV)
    picked = jnp.where(position < SUBS, which, -1)
    return picked.T.astype(jnp.int32)


def draw_unique_q(key, part):
    values = 3.0 * jnp.clip(jax.random.normal(jax.random.fold_in(key, 13), (ROWS, QW), jnp.float32), -6.0, 6.0)
    return values.astype(jnp.bfloat16)


def draw_unique_kv(key, part):
    values = jnp.clip(jax.random.normal(jax.random.fold_in(key, 17), (ROWS, 2 * KVW), jnp.float32), -6.0, 6.0)
    return values.astype(jnp.bfloat16)


def block_scale(stream_key, dims, cuts, least, top_value):
    level = 1.0
    for dim, shards_of in cuts:
        steps = jax.random.uniform(jax.random.fold_in(jax.random.fold_in(stream_key, 6), dim), (shards_of,), jnp.float32, least / len(cuts), top_value / len(cuts))
        level = level * jnp.repeat(jnp.exp(steps), dims[dim] // shards_of).reshape((-1,) + (1,) * (len(dims) - 1 - dim))
    return level


def split_up(amount, total, reach, skew):
    portions = [(1 << 20) // math.isqrt(rank ** skew) + 1 for rank in range(2, amount + 1)]
    surplus, counts = total - reach - (amount - 1), [1] * (amount - 1)
    while surplus > 0:
        candidates = [i for i in range(amount - 1) if counts[i] < reach]
        mass, budget = sum([portions[i] for i in candidates]), surplus
        for i in candidates:
            more = min(reach - counts[i], max(1, budget * portions[i] // mass), surplus)
            counts[i] = counts[i] + more
            surplus = surplus - more
    return np.array([reach] + counts)


def ragged_sizes(stream_key, number_of, total, most, slope):
    if number_of == 2:
        one = jax.random.randint(stream_key, (), max(1, total - most), min(most, total - 1) + 1)
        return jnp.stack([one, total - one])
    sizes = jnp.asarray(split_up(number_of, total, most, slope), jnp.int32)
    pairs = (number_of - 1) // 2
    source_of, sink = sizes[1:1 + 2 * pairs:2], sizes[2:2 + 2 * pairs:2]
    margin = jnp.minimum(source_of - 1, most - sink)
    shifted = jax.random.randint(jax.random.fold_in(stream_key, 1), (pairs,), 0, 1 << 20) % (margin + 1)
    sizes = sizes.at[1:1 + 2 * pairs:2].set(source_of - shifted).at[2:2 + 2 * pairs:2].set(sink + shifted)
    return sizes[jax.random.permutation(jax.random.fold_in(stream_key, 2), number_of)]


def shared_out(stream_key, own, number, rows, number_of, top, reach, lean):
    sequence = jax.random.permutation(stream_key, number_of)
    packed, ordinary = load_shares(number_of, rows * top, reach, lean, True), load_shares(number_of, rows * top, reach, lean, False)
    places = jnp.arange(number_of)

    def named(lengths, turn):
        used = int((lengths > 0).sum())
        fixed = max(1, used // 4)
        passed = fixed + (places - fixed + turn * (used - fixed)) % max(1, number_of - fixed)
        return jnp.zeros((number_of,), jnp.int32).at[sequence[jnp.where(places < fixed, places, passed)]].set(jnp.asarray(lengths, jnp.int32))

    lengths = jnp.where(number % 4 == 0, named(packed, number // 4), named(ordinary, number - number // 4 - 1))
    mixed = jax.random.permutation(jax.random.fold_in(own, 3), number_of)
    source_of, taker = mixed[0:number_of // 2 * 2:2], mixed[1:number_of // 2 * 2:2]
    slack = jnp.minimum(lengths[source_of] - 1, reach - lengths[taker]) // 2
    slack = jnp.where((source_of == sequence[0]) | (taker == sequence[0]) | (lengths[taker] == 0), 0, jnp.maximum(slack, 0))
    passed = jax.random.randint(jax.random.fold_in(own, 4), (number_of // 2,), 0, 1 << 20) % (slack + 1)
    lengths = lengths.at[source_of].add(-passed).at[taker].add(passed)
    labels = jnp.searchsorted(jnp.cumsum(lengths), jnp.arange(rows * top), side="right").astype(jnp.int32)
    grid = labels.reshape(top, rows).T
    grid = grid[jax.random.permutation(jax.random.fold_in(own, 1), rows)]
    turn = jax.random.randint(jax.random.fold_in(own, 2), (rows, 1), 0, top)
    return jnp.take_along_axis(grid, (jnp.arange(top)[None, :] + turn) % top, axis=1)


def load_shares(count, total, reach, lean, full):
    loads = [(1 << 20) // math.isqrt(rank ** lean) + 1 for rank in range(1, count + 1)]
    largest = reach if full else min(reach, max(-(-total // count), total * loads[0] // sum(loads)))
    least = 1 if total - largest >= count - 1 else 0
    counts, surplus = [largest] + [least] * (count - 1), total - largest - least * (count - 1)
    while surplus > 0:
        candidates = [i for i in range(1, count) if counts[i] < largest] or [i for i in range(1, count) if counts[i] < reach]
        mass, left = sum([loads[i] for i in candidates]), surplus
        for i in candidates:
            more = min(reach - counts[i], max(1, left * loads[i] // mass), surplus)
            counts[i] = counts[i] + more
            surplus = surplus - more
    return np.array(counts)


def normal_values(key, shape, scale, limit, pieces=(), held_as=jnp.bfloat16):
    array = jax.random.normal(key, shape, jnp.float32) * scale
    if len(pieces) > 0:
        array = block_scale(key, shape, pieces, -0.22, 0.18) * array
    return jnp.clip(array, min=-limit, max=limit).astype(held_as)


def setup_inputs(seed: int = 0, part: int = 0) -> dict:
    key_of = jax.random.split(jax.random.key(seed), 10)
    own_keys = jax.random.split(jax.random.fold_in(key_of[9], part), 10)
    prompt_k = draw_prompt_k(jax.random.fold_in(jax.random.fold_in(key_of[9], part), 71), part)
    prompt_v = normal_values(own_keys[1], (N_BRANCH, PLEN, KVW), 1.0, 6.0, ((0, 16),))
    prompt_mask = draw_prompt_mask(jax.random.fold_in(jax.random.fold_in(key_of[9], part), 71), part)
    shared_kv = normal_values(own_keys[3], (NRES, RLEN, 2 * KVW), 1.0, 6.0, ((0, 16),))
    shared_len = ragged_sizes(own_keys[4], NRES, NRES * (RLEN + 1) // 2, RLEN, 2).astype(jnp.int32)
    send_pick = draw_send_pick(jax.random.fold_in(jax.random.fold_in(key_of[9], part), 71), part)
    unique_q = draw_unique_q(jax.random.fold_in(jax.random.fold_in(key_of[9], part), 71), part)
    unique_kv = draw_unique_kv(jax.random.fold_in(jax.random.fold_in(key_of[9], part), 71), part)
    unique_owner_keys = jax.random.split(jax.random.fold_in(own_keys[8], 1), ROWS // UNQ_DEV)
    unique_owner_turns = jax.random.permutation(jax.random.fold_in(own_keys[8], 3), ROWS // UNQ_DEV)
    unique_owner = jax.vmap(lambda own, number: shared_out(jax.random.fold_in(own_keys[8], 2), own, number, UNQ_DEV, N_BRANCH, 1, CAP, 2))(unique_owner_keys, unique_owner_turns).reshape((ROWS, 1))
    return {"prompt_k": prompt_k, "prompt_v": prompt_v, "prompt_mask": prompt_mask, "shared_kv": shared_kv, "shared_len": shared_len, "send_pick": send_pick, "unique_q": unique_q, "unique_kv": unique_kv, "unique_owner": unique_owner}


def attend(queries, key_rows, value_rows, allowed):
    count = queries.shape[0]
    keys_total = key_rows.shape[0]
    grouped = queries.reshape(count, KVH, GRP, HD).transpose(1, 2, 0, 3).astype(jnp.float32)
    key_heads = key_rows.reshape(keys_total, KVH, HD).transpose(1, 0, 2).astype(jnp.float32)
    value_heads = value_rows.reshape(keys_total, KVH, HD).transpose(1, 0, 2).astype(jnp.float32)
    scale = 1.0 / math.sqrt(HD)

    def one_head(operands):
        query_group, key_group, value_group = operands
        scores = jnp.einsum('gsd,kd->gsk', query_group, key_group) * scale
        scores = jnp.where(allowed[None], scores, -1e+30)
        largest = lax.optimization_barrier(jnp.max(scores, axis=-1, keepdims=True))
        weights = jnp.exp(scores - largest)
        total = lax.optimization_barrier(jnp.sum(weights, axis=-1, keepdims=True))
        probs = lax.optimization_barrier(weights.astype(jnp.bfloat16)).astype(jnp.float32)
        mixed = jnp.einsum('gsk,kd->gsd', probs, value_group)
        return (mixed / total).astype(jnp.bfloat16)
    heads = lax.map(one_head, (grouped, key_heads, value_heads))
    return heads.transpose(2, 0, 1, 3).reshape(count, QH * HD)

def reference(prompt_k, prompt_v, prompt_mask, shared_kv, shared_len, send_pick, unique_q, unique_kv, unique_owner):
    owner_of = unique_owner[:, 0].astype(jnp.int32)
    positions = jnp.arange(ROWS, dtype=jnp.int32)
    source = positions // UNQ_DEV
    grid_owner = owner_of.reshape(N_BRANCH, UNQ_DEV)
    in_device = jnp.arange(UNQ_DEV, dtype=jnp.int32)
    earlier = (grid_owner[:, :, None] == grid_owner[:, None, :]) & (in_device[None, None, :] < in_device[None, :, None])
    rank = lax.optimization_barrier(jnp.sum(earlier.astype(jnp.int32), axis=2)).reshape(ROWS).astype(jnp.int32)
    slot_index = (source * CAP + rank).astype(jnp.int32)
    width = N_BRANCH * CAP
    query_slots = jnp.zeros((N_BRANCH, width, QW), jnp.bfloat16).at[owner_of, slot_index].set(unique_q)
    pair_slots = jnp.zeros((N_BRANCH, width, 2 * KVW), jnp.bfloat16).at[owner_of, slot_index].set(unique_kv)
    live_slots = jnp.zeros((N_BRANCH, width), jnp.int32).at[owner_of, slot_index].set(1)
    by_owner = shared_kv.reshape(N_BRANCH, RES_DEV, RLEN, 2 * KVW)
    len_by_owner = shared_len.reshape(N_BRANCH, RES_DEV)
    owners = jnp.arange(N_BRANCH, dtype=jnp.int32)
    within = jnp.arange(RLEN, dtype=jnp.int32)
    slot_range = jnp.arange(width, dtype=jnp.int32)
    causal = slot_range[None, :] <= slot_range[:, None]

    def one_branch(branch_id):
        picked = send_pick[:, branch_id]
        safe = jnp.maximum(picked, 0).astype(jnp.int32)
        fetched = by_owner[owners, safe].reshape(N_BRANCH * RLEN, 2 * KVW)
        live_len = jnp.where(picked >= 0, len_by_owner[owners, safe], 0)
        shared_ok = (within[None, :] < live_len[:, None]).reshape(N_BRANCH * RLEN)
        block_ok = jnp.repeat(prompt_mask[branch_id] > 0, PB)
        unique_ok = causal & (live_slots[branch_id] > 0)[None, :]
        allowed = jnp.concatenate([jnp.broadcast_to(block_ok[None], (width, PLEN)), jnp.broadcast_to(shared_ok[None], (width, N_BRANCH * RLEN)), unique_ok], axis=1)
        pairs = pair_slots[branch_id]
        key_rows = jnp.concatenate([prompt_k[branch_id], fetched[:, :KVW], pairs[:, :KVW]], axis=0)
        value_rows = jnp.concatenate([prompt_v[branch_id], fetched[:, KVW:], pairs[:, KVW:]], axis=0)
        return attend(query_slots[branch_id], key_rows, value_rows, allowed)
    results = lax.map(one_branch, owners)
    return results[owner_of, slot_index]
```

```python
import functools
import math

import jax
import jax.numpy as jnp
from jax import lax
from jax.experimental import pallas as pl
from jax.experimental.pallas import tpu as pltpu
from jax.sharding import PartitionSpec as P

HD = 128
GRP = 8
CAP = 2
TILE = 16
NONE = -1e30
ABSENT = 512.0
VMEM = pl.BlockSpec(memory_space=pltpu.VMEM)
SMEM = pl.BlockSpec(memory_space=pltpu.SMEM)


def payload_kernel(pick_ref, len_ref, shared_ref, out_ref):
    results, rows, width = shared_ref.shape
    branches = pick_ref.shape[1]
    lane = lax.broadcasted_iota(jnp.int32, (TILE, HD), 1)
    meta = jnp.zeros((TILE, HD), jnp.int32)
    for b in range(branches):
        meta = jnp.where(lane == b, pick_ref[0, b], meta)
    for r in range(results):
        meta = jnp.where(lane == branches + r, len_ref[r], meta)
    out_ref[0:TILE, :] = meta.astype(jnp.float32).astype(jnp.bfloat16)
    live = results * rows
    for j in range(width // HD):
        part = shared_ref[:, :, j * HD : (j + 1) * HD].astype(jnp.float32)
        out_ref[TILE + j * live : TILE + (j + 1) * live, :] = part.reshape(live, HD).astype(jnp.bfloat16)


def place_rows(owner_ref, index_ref, count_ref):
    branches = count_ref.shape[0]
    for b in range(branches):
        count_ref[b] = 0
    for i in range(owner_ref.shape[0]):
        b = owner_ref[i]
        rank = count_ref[b]
        if index_ref is not None:
            index_ref[b * CAP + rank] = i
        count_ref[b] = rank + 1


def prep_kernel(owner_ref, q_ref, kv_ref, out_ref, index_ref, count_ref, q3_ref, kv3_ref):
    rows, q_width = q_ref.shape
    branches = out_ref.shape[0]
    heads = q_width // HD
    kv_heads = heads // GRP
    for b in range(branches * CAP):
        index_ref[b] = 0
    place_rows(owner_ref, index_ref, count_ref)
    q3_ref[...] = q_ref[...].astype(jnp.float32).reshape(rows, heads, HD)
    kv3_ref[...] = kv_ref[...].astype(jnp.float32).reshape(rows, 2 * kv_heads, HD)

    @pl.loop(0, branches)
    def _(b):
        index = [index_ref[b * CAP + c] for c in range(CAP)]
        parts = [q3_ref[i].reshape(kv_heads, 1, GRP, HD) for i in index]
        tiles = jnp.concatenate(parts, axis=1).reshape(heads * CAP, HD)
        pairs = [kv3_ref[i] for i in index]
        there = [count_ref[b] > c for c in range(CAP)]
        keys = [jnp.where(t, p[:kv_heads], ABSENT) for t, p in zip(there, pairs)]
        values = [jnp.where(t, p[kv_heads:], 0.0) for t, p in zip(there, pairs)]
        out_ref[b] = jnp.concatenate([tiles] + keys + values, axis=0).astype(jnp.bfloat16)


def attend_kernel(full, split, me_ref, mask_ref, pk_ref, pv_ref, recv_ref, *refs):
    out_ref = refs[-1]
    blocks = [(ref, ref, TILE * 1) for ref in refs[:full]]
    halves = refs[full : full + 2 * split]
    blocks += [(halves[2 * i], halves[2 * i + 1], 0) for i in range(split)]
    branches = recv_ref.shape[0]
    kv_heads = pk_ref.shape[2] // HD
    prompt = pk_ref.shape[1]
    width = branches * CAP
    live = (refs[0].shape[0] - TILE) // (2 * kv_heads)
    rows = live // 2
    heads = kv_heads * GRP
    factor = math.log2(math.e) / math.sqrt(HD)
    me = me_ref[0]

    lane = lax.broadcasted_iota(jnp.int32, (1, HD), 1)
    column = lax.broadcasted_iota(jnp.int32, (1, live), 1)
    biases = []
    for key_ref, _, _ in blocks:
        meta = key_ref[0:TILE, :].astype(jnp.float32)[0:1, :]
        pick = jnp.sum(jnp.where(lane == me, meta, 0.0), axis=1, keepdims=True)
        ok = jnp.zeros((1, live), jnp.bool_)
        for r in range(2):
            length = jnp.sum(jnp.where(lane == branches + r, meta, 0.0), axis=1, keepdims=True)
            place = (column - r * rows).astype(jnp.float32)
            ok = ok | ((place >= 0.0) & (place < length) & (pick == float(r)))
        biases.append(jnp.where(ok, 0.0, NONE))
    shared_bias = jnp.concatenate(biases, axis=1)

    blocks_seen = mask_ref.shape[1]
    span = prompt // blocks_seen
    prompt_bias = jnp.concatenate(
        [jnp.full((1, span), jnp.where(mask_ref[0, j] > 0, 0.0, NONE)) for j in range(blocks_seen)], axis=1
    )

    all_keys = recv_ref[:, heads * CAP : heads * CAP + TILE, :].reshape(branches * TILE, HD)
    all_values = recv_ref[:, heads * CAP + TILE : heads * CAP + 2 * TILE, :].reshape(branches * TILE, HD)
    chunk = min(branches, 16)
    chunk_rows = chunk * CAP * GRP
    nt = (((1,), (1,)), ((), ()))

    @pl.loop(0, kv_heads)
    def _(g):
        at = pl.multiple_of(g * HD, HD)
        spot = pl.multiple_of(g * live, TILE)
        prompt_keys = pk_ref[0, :, pl.ds(at, HD)]
        prompt_values = pv_ref[0, :, pl.ds(at, HD)]
        shared_keys = jnp.concatenate([k[pl.ds(TILE + spot, live), :] for k, _, _ in blocks], axis=0)
        shared_values = jnp.concatenate(
            [v[pl.ds((TILE + kv_heads * live if whole else 0) + spot, live), :] for _, v, whole in blocks], axis=0
        )
        place = lax.broadcasted_iota(jnp.int32, (width, branches * TILE), 1)
        slot = lax.broadcasted_iota(jnp.int32, (width, branches * TILE), 0)
        choose = jnp.where(place == slot * kv_heads + g, 1.0, 0.0).astype(jnp.bfloat16)
        keys = jnp.dot(choose, all_keys, preferred_element_type=jnp.float32).astype(jnp.bfloat16)
        values = jnp.dot(choose, all_values, preferred_element_type=jnp.float32).astype(jnp.bfloat16)
        first = jnp.where(lax.broadcasted_iota(jnp.int32, (TILE, HD), 1) == 0, 1.0, 0.0).astype(jnp.bfloat16)
        flag = lax.dot_general(first, keys, nt, preferred_element_type=jnp.float32)[0:1, :]

        @pl.loop(0, branches // chunk)
        def _(part):
            base = part * chunk
            queries = recv_ref[pl.ds(base, chunk), pl.ds(pl.multiple_of(g * TILE, TILE), TILE), :]
            queries = queries.reshape(chunk_rows, HD)

            def scores(k):
                return lax.dot_general(queries, k, nt, preferred_element_type=jnp.float32)

            own_slot = base * CAP + lax.broadcasted_iota(jnp.int32, (chunk_rows, width), 0) // GRP
            key_slot = lax.broadcasted_iota(jnp.int32, (chunk_rows, width), 1)
            seen = (key_slot <= own_slot) & (flag < ABSENT / 2)
            sets = [
                (scores(prompt_keys) + prompt_bias, prompt_values),
                (scores(shared_keys) + shared_bias, shared_values),
                (jnp.where(seen, scores(keys), NONE), values),
            ]
            largest = functools.reduce(
                jnp.maximum, [jnp.max(s, axis=1, keepdims=True) for s, _ in sets]
            )
            total = jnp.zeros((chunk_rows, 1), jnp.float32)
            mixed = jnp.zeros((chunk_rows, HD), jnp.float32)
            for s, v in sets:
                weights = jnp.exp2((s - largest) * factor)
                total = total + jnp.sum(weights, axis=1, keepdims=True)
                mixed = mixed + jnp.dot(weights.astype(jnp.bfloat16), v, preferred_element_type=jnp.float32)
            result = (mixed / total).astype(jnp.bfloat16)
            out_ref[pl.ds(base, chunk), pl.ds(pl.multiple_of(g * TILE, TILE), TILE), :] = result.reshape(
                chunk, TILE, HD
            )


def post_kernel(owner_ref, back_ref, out_ref, count_ref, o3_ref):
    rows, width = out_ref.shape
    heads = width // HD
    branches = back_ref.shape[0]
    for b in range(branches):
        count_ref[b] = 0

    @pl.loop(0, rows)
    def _(i):
        b = owner_ref[i]
        rank = count_ref[b]
        count_ref[b] = rank + 1
        tiles = back_ref[b].astype(jnp.float32).reshape(heads // GRP, CAP, GRP, HD)
        o3_ref[i] = jnp.where(rank == 0, tiles[:, 0], tiles[:, 1]).reshape(heads, HD)

    out_ref[...] = o3_ref[...].reshape(rows, width).astype(jnp.bfloat16)


def body(
    prompt_k, prompt_v, prompt_mask, shared_kv, shared_len, send_pick, unique_q, unique_kv, unique_owner
):
    branches = lax.axis_size("branch")
    chips = branches // 2
    row_count, q_width = unique_q.shape
    heads = q_width // HD
    kv_width = unique_kv.shape[1] // 2
    kv_heads = kv_width // HD
    results, result_rows, _ = shared_kv.shape
    owner_of = unique_owner[:, 0]
    live = results * result_rows
    payload_rows = TILE + 2 * kv_heads * live
    slot_rows = CAP * heads + 2 * TILE
    params = pltpu.CompilerParams(vmem_limit_bytes=32 << 20)

    payload = pl.pallas_call(
        payload_kernel,
        out_shape=jax.ShapeDtypeStruct((payload_rows, HD), jnp.bfloat16),
        in_specs=[SMEM, SMEM, VMEM],
        out_specs=VMEM,
        compiler_params=params,
        name="payload",
    )(send_pick, shared_len, shared_kv)
    send = pl.pallas_call(
        prep_kernel,
        out_shape=jax.ShapeDtypeStruct((branches, slot_rows, HD), jnp.bfloat16),
        in_specs=[SMEM, VMEM, VMEM],
        out_specs=VMEM,
        scratch_shapes=[
            pltpu.SMEM((branches * CAP,), jnp.int32),
            pltpu.SMEM((branches,), jnp.int32),
            pltpu.VMEM((row_count, heads, HD), jnp.float32),
            pltpu.VMEM((row_count, 2 * kv_heads, HD), jnp.float32),
        ],
        compiler_params=params,
        name="prep",
    )(owner_of, unique_q, unique_kv)
    recv = lax.all_to_all(send, "branch", split_axis=0, concat_axis=0, tiled=True)

    order = list(range(0, chips, 2)) + list(range(1, chips, 2))[::-1]

    def along(x, step):
        pairs = [
            (order[p] * 2 + core, order[(p + step) % chips] * 2 + core)
            for p in range(chips)
            for core in range(2)
        ]
        return lax.ppermute(x, "branch", pairs)

    def across(x):
        return lax.ppermute(x, "branch", [(i, i ^ 1) for i in range(branches)])

    cut = TILE + kv_heads * live
    whole = [payload]
    ahead = behind = payload
    for _ in range(chips // 2 - 1):
        ahead, behind = along(ahead, 1), along(behind, -1)
        whole += [ahead, behind]
    last = [along(ahead[:cut], 1), along(behind[cut:], -1)]
    blocks = whole + [across(x) for x in whole]
    halves = last + [across(x) for x in last]
    me = jnp.full((1,), lax.axis_index("branch"), jnp.int32)
    keys = prompt_k.shape[1] + branches * live + CAP * branches
    outputs = pl.pallas_call(
        functools.partial(attend_kernel, len(blocks), len(halves) // 2),
        out_shape=jax.ShapeDtypeStruct((branches, CAP * heads, HD), jnp.bfloat16),
        in_specs=[SMEM, SMEM] + [VMEM] * (3 + len(blocks) + len(halves)),
        out_specs=VMEM,
        compiler_params=params,
        cost_estimate=pl.CostEstimate(
            flops=4 * branches * CAP * heads * HD * keys,
            bytes_accessed=4 * prompt_k.size,
            transcendentals=branches * CAP * heads * keys,
        ),
        name="attend",
    )(me, prompt_mask, prompt_k, prompt_v, recv, *blocks, *halves)
    back = lax.all_to_all(outputs, "branch", split_axis=0, concat_axis=0, tiled=True)
    return pl.pallas_call(
        post_kernel,
        out_shape=jax.ShapeDtypeStruct((row_count, q_width), jnp.bfloat16),
        in_specs=[SMEM, VMEM],
        out_specs=VMEM,
        scratch_shapes=[
            pltpu.SMEM((branches,), jnp.int32),
            pltpu.VMEM((row_count, heads, HD), jnp.float32),
        ],
        compiler_params=params,
        name="post",
    )(owner_of, back)


def solution(mesh):
    split = ("groups", "branch")
    in_specs = (
        P(split, None, None),
        P(split, None, None),
        P(split, None),
        P(split, None, None),
        P(split),
        P(split, None),
        P(split, None),
        P(split, None),
        P(split, None),
    )
    return jax.shard_map(body, mesh=mesh, in_specs=in_specs, out_specs=P(split, None), check_vma=False)
```

```python
import functools
import math

import jax
import jax.numpy as jnp
from jax import lax
from jax.experimental import pallas as pl
from jax.experimental.pallas import tpu as pltpu
from jax.sharding import PartitionSpec as P

HD = 128
GRP = 8
CAP = 2
TILE = 16
NONE = -1e30
ABSENT = 512.0
VMEM = pl.BlockSpec(memory_space=pltpu.VMEM)
SMEM = pl.BlockSpec(memory_space=pltpu.SMEM)
ANY = pl.BlockSpec(memory_space=pl.ANY)


def grant(mebibytes):
    return pltpu.CompilerParams(vmem_limit_bytes=mebibytes << 20)


def payload_kernel(pick_hbm, len_hbm, shared_hbm, out_ref, pick_ref, len_ref, shared_ref, sems):
    results, rows, width = shared_ref.shape
    branches = pick_ref.shape[1]
    moves = [
        pltpu.make_async_copy(source, target, sems.at[n])
        for n, (source, target) in enumerate(
            ((shared_hbm, shared_ref), (pick_hbm, pick_ref), (len_hbm, len_ref))
        )
    ]
    for move in moves:
        move.start()
    for move in moves:
        move.wait()
    live = results * rows
    lane = lax.broadcasted_iota(jnp.int32, (live, HD), 1)
    meta = jnp.zeros((live, HD), jnp.int32)
    for b in range(branches):
        meta = jnp.where(lane == b, pick_ref[0, b], meta)
    for r in range(results):
        meta = jnp.where(lane == branches + r, len_ref[0, r], meta)
    slabs = width // HD
    out_ref[slabs] = meta.astype(jnp.float32).astype(jnp.bfloat16)
    for j in range(slabs):
        part = shared_ref[:, :, j * HD : (j + 1) * HD].astype(jnp.float32)
        out_ref[j] = part.reshape(live, HD).astype(jnp.bfloat16)


def place_rows(owner_ref, index_ref, count_ref):
    branches = count_ref.shape[0]
    for b in range(branches):
        count_ref[b] = 0
    for i in range(owner_ref.shape[0]):
        b = owner_ref[i]
        rank = count_ref[b]
        if index_ref is not None:
            index_ref[b * CAP + rank] = i
        count_ref[b] = rank + 1


def prep_kernel(owner_ref, q_hbm, kv_hbm, after_hbm, out_ref, index_ref, count_ref, q_ref, kv_ref, q3_ref, kv3_ref, sems):
    del after_hbm
    rows, q_width = q_ref.shape
    branches = out_ref.shape[0]
    heads = q_width // HD
    kv_heads = heads // GRP
    moves = [
        pltpu.make_async_copy(q_hbm, q_ref, sems.at[0]),
        pltpu.make_async_copy(kv_hbm, kv_ref, sems.at[1]),
    ]
    for move in moves:
        move.start()
    for b in range(branches * CAP):
        index_ref[b] = 0
    place_rows(owner_ref, index_ref, count_ref)
    for move in moves:
        move.wait()
    q3_ref[...] = q_ref[...].astype(jnp.float32).reshape(rows, heads, HD)
    kv3_ref[...] = kv_ref[...].astype(jnp.float32).reshape(rows, 2 * kv_heads, HD)

    @pl.loop(0, branches)
    def _(b):
        index = [index_ref[b * CAP + c] for c in range(CAP)]
        parts = [q3_ref[i].reshape(kv_heads, 1, GRP, HD) for i in index]
        tiles = jnp.concatenate(parts, axis=1).reshape(heads * CAP, HD)
        pairs = [kv3_ref[i] for i in index]
        there = [count_ref[b] > c for c in range(CAP)]
        keys = [jnp.where(t, p[:kv_heads], ABSENT) for t, p in zip(there, pairs)]
        values = [jnp.where(t, p[kv_heads:], 0.0) for t, p in zip(there, pairs)]
        out_ref[b] = jnp.concatenate([tiles] + keys + values, axis=0).astype(jnp.bfloat16)


def dot_nt(a, b):
    return lax.dot_general(a, b, (((1,), (1,)), ((), ())), preferred_element_type=jnp.float32)


FACTOR = math.log2(math.e) / math.sqrt(HD)


def starter(sems):
    free = iter(range(sems.shape[0]))

    def start(source, target):
        copy = pltpu.make_async_copy(source, target, sems.at[next(free)])
        copy.start()
        return copy

    return start


def bias_of(meta, me, branches, live):
    lane = lax.broadcasted_iota(jnp.int32, (1, HD), 1)
    column = lax.broadcasted_iota(jnp.int32, (1, live), 1)
    rows = live // 2
    pick = jnp.sum(jnp.where(lane == me, meta, 0.0), axis=1, keepdims=True)
    seen = jnp.zeros((1, live), jnp.bool_)
    for r in range(2):
        length = jnp.sum(jnp.where(lane == branches + r, meta, 0.0), axis=1, keepdims=True)
        place = (column - r * rows).astype(jnp.float32)
        seen = seen | ((place >= 0.0) & (place < length) & (pick == float(r)))
    return jnp.where(seen, 0.0, NONE)


def gather_kernel(whole, branches, me_ref, mask_ref, pk_hbm, pv_hbm, *refs):
    blocks = refs[:whole]
    key_ref, value_hbm, bias_ref, value_ref, meta_ref, sems = refs[whole:]
    kv_heads = key_ref.shape[0]
    prompt = pk_hbm.shape[1]
    live = meta_ref.shape[1]
    start = starter(sems)
    moves, metas = [], []
    for n, block in enumerate(blocks):
        span = pl.ds(prompt + n * live, live)
        metas.append(start(block.at[2 * kv_heads], meta_ref.at[n]))
        moves.append(start(block.at[kv_heads : 2 * kv_heads], value_ref.at[:, span, :]))
        moves.append(start(block.at[0:kv_heads], key_ref.at[:, span, :]))
    for g in range(kv_heads):
        lanes = pl.ds(g * HD, HD)
        moves.append(start(pv_hbm.at[0, :, lanes], value_ref.at[g, pl.ds(0, prompt), :]))
        moves.append(start(pk_hbm.at[0, :, lanes], key_ref.at[g, pl.ds(0, prompt), :]))
    for copy in metas:
        copy.wait()
    seen = mask_ref.shape[1]
    biases = [
        jnp.full((1, prompt // seen), jnp.where(mask_ref[0, j] > 0, 0.0, NONE)) for j in range(seen)
    ]
    for n in range(whole):
        meta = meta_ref[n, 0:TILE, :].astype(jnp.float32)[0:1, :]
        biases.append(bias_of(meta, me_ref[0], branches, live))
    bias = jnp.concatenate(biases, axis=1)
    bias_ref[...] = jnp.broadcast_to(bias, bias_ref.shape)
    for copy in moves:
        copy.wait()
    leaving = start(value_ref, value_hbm)
    leaving.wait()


def attend_kernel(
    split, me_ref, key_ref, bias_ref, value_hbm, recv_hbm, *refs
):
    out_ref, late_key_ref, late_value_ref, first_ref, second_ref, value_ref, recv_ref = refs[
        2 * split : 2 * split + 7
    ]
    halves, sems = refs[2 * split + 7 : -1], refs[-1]
    kv_heads = key_ref.shape[0]
    start = starter(sems)
    rows_move = start(recv_hbm, recv_ref)
    half_moves = [start(source, target) for source, target in zip(refs[: 2 * split], halves)]
    value_moves = [start(value_hbm.at[g], value_ref.at[g]) for g in range(kv_heads)]
    branches = recv_ref.shape[0]
    heads = kv_heads * GRP
    width = branches * CAP
    early = key_ref.shape[1]
    late = late_key_ref.shape[1]
    live = halves[0].shape[1]
    far = split * live

    chunk = min(branches, 16)
    count = chunk * TILE

    def score(g, base, target):
        queries = recv_ref[pl.ds(base, chunk), g * TILE : (g + 1) * TILE, :].reshape(count, HD)
        target[:, 0:early] = dot_nt(queries, key_ref[g]) + bias_ref[0:1, :]

    rows_move.wait()
    if branches == chunk:
        score(0, 0, first_ref)
    for copy in half_moves:
        copy.wait()

    late_bias = [
        bias_of(halves[2 * n][kv_heads, 0:TILE, :].astype(jnp.float32)[0:1, :], me_ref[0], branches, live)
        for n in range(split)
    ]
    late_bias = jnp.concatenate(late_bias + [jnp.zeros((1, width), jnp.float32)], axis=1)
    size = branches * TILE
    place = lax.broadcasted_iota(jnp.int32, (size, size), 1)
    wanted = lax.broadcasted_iota(jnp.int32, (size, size), 0)
    choose = jnp.where(place == lax.rem(wanted, width) * kv_heads + wanted // width, 1.0, 0.0).astype(jnp.bfloat16)
    for which, target in ((0, late_key_ref), (1, late_value_ref)):
        first = heads * CAP + which * TILE
        rows = recv_ref[:, first : first + TILE, :].reshape(size, HD)
        rows = jnp.dot(choose, rows, preferred_element_type=jnp.float32).astype(jnp.bfloat16)
        target[:, far:late, :] = rows.reshape(kv_heads, width, HD)
        for n in range(split):
            target[:, n * live : (n + 1) * live, :] = halves[2 * n + which][0:kv_heads]
    one = jnp.where(lax.broadcasted_iota(jnp.int32, (TILE, HD), 1) == 0, 1.0, 0.0).astype(jnp.bfloat16)
    absent = dot_nt(one, late_key_ref[0])[0:1, :] > ABSENT / 2
    for copy in value_moves:
        copy.wait()

    column = lax.broadcasted_iota(jnp.int32, (count, late), 1) - far
    own_slot = lax.broadcasted_iota(jnp.int32, (count, late), 0) // GRP

    def run(base):
        late_hidden = jnp.where((column >= 0) & (absent | (column > own_slot + base * CAP)), NONE, late_bias)

        def score_late(g, target):
            queries = recv_ref[pl.ds(base, chunk), g * TILE : (g + 1) * TILE, :].reshape(count, HD)
            target[:, early : early + late] = dot_nt(queries, late_key_ref[g]) + late_hidden

        def finish(g, source):
            scores = source[...]
            largest = jnp.max(scores, axis=1, keepdims=True)
            weights = jnp.exp2((scores - largest) * FACTOR)
            total = jnp.sum(weights, axis=1, keepdims=True)
            probs = weights.astype(jnp.bfloat16)
            mixed = jnp.dot(probs[:, 0:early], value_ref[g], preferred_element_type=jnp.float32)
            mixed = mixed + jnp.dot(probs[:, early:], late_value_ref[g], preferred_element_type=jnp.float32)
            result = (mixed / total).astype(jnp.bfloat16)
            out_ref[pl.ds(base, chunk), g * TILE : (g + 1) * TILE, :] = result.reshape(chunk, TILE, HD)

        buffers = (first_ref, second_ref)
        if branches > chunk:
            score(0, base, buffers[0])
        score_late(0, buffers[0])
        for g in range(kv_heads):
            if g + 1 < kv_heads:
                score(g + 1, base, buffers[(g + 1) % 2])
                score_late(g + 1, buffers[(g + 1) % 2])
            finish(g, buffers[g % 2])

    if branches == chunk:
        run(0)
    else:
        @pl.loop(0, branches // chunk)
        def _(part):
            run(part * chunk)


def post_kernel(owner_ref, back_ref, out_ref, count_ref, o3_ref):
    rows, width = out_ref.shape
    heads = width // HD
    branches = back_ref.shape[0]
    for b in range(branches):
        count_ref[b] = 0

    @pl.loop(0, rows)
    def _(i):
        b = owner_ref[i]
        rank = count_ref[b]
        count_ref[b] = rank + 1
        tiles = back_ref[b].astype(jnp.float32).reshape(heads // GRP, CAP, GRP, HD)
        o3_ref[i] = jnp.where(rank == 0, tiles[:, 0], tiles[:, 1]).reshape(heads, HD)

    out_ref[...] = o3_ref[...].reshape(rows, width).astype(jnp.bfloat16)


def body(
    prompt_k, prompt_v, prompt_mask, shared_kv, shared_len, send_pick, unique_q, unique_kv, unique_owner
):
    branches = lax.axis_size("branch")
    chips = branches // 2
    row_count, q_width = unique_q.shape
    heads = q_width // HD
    kv_width = unique_kv.shape[1] // 2
    kv_heads = kv_width // HD
    results, result_rows, _ = shared_kv.shape
    owner_of = unique_owner[:, 0]
    live = results * result_rows
    slot_rows = CAP * heads + 2 * TILE

    def bf16(*shape):
        return jax.ShapeDtypeStruct(shape, jnp.bfloat16)

    block = pl.pallas_call(
        payload_kernel,
        out_shape=bf16(2 * kv_heads + 1, live, HD),
        in_specs=[ANY] * 3,
        out_specs=VMEM,
        scratch_shapes=[
            pltpu.SMEM(send_pick.shape, jnp.int32),
            pltpu.SMEM((1, results), jnp.int32),
            pltpu.VMEM(shared_kv.shape, jnp.bfloat16),
            pltpu.SemaphoreType.DMA((3,)),
        ],
        compiler_params=grant(56),
        name="payload",
    )(send_pick, shared_len.reshape(1, results), shared_kv)

    order = list(range(0, chips, 2)) + list(range(1, chips, 2))[::-1]

    def along(x, step):
        pairs = [
            (order[p] * 2 + core, order[(p + step) % chips] * 2 + core)
            for p in range(chips)
            for core in range(2)
        ]
        return lax.ppermute(x, "branch", pairs)

    def across(x):
        return lax.ppermute(x, "branch", [(i, i ^ 1) for i in range(branches)])

    send = pl.pallas_call(
        prep_kernel,
        out_shape=bf16(branches, slot_rows, HD),
        in_specs=[SMEM, ANY, ANY, ANY],
        out_specs=VMEM,
        scratch_shapes=[
            pltpu.SMEM((branches * CAP,), jnp.int32),
            pltpu.SMEM((branches,), jnp.int32),
            pltpu.VMEM(unique_q.shape, jnp.bfloat16),
            pltpu.VMEM(unique_kv.shape, jnp.bfloat16),
            pltpu.VMEM((row_count, heads, HD), jnp.float32),
            pltpu.VMEM((row_count, 2 * kv_heads, HD), jnp.float32),
            pltpu.SemaphoreType.DMA((2,)),
        ],
        compiler_params=grant(56),
        cost_estimate=pl.CostEstimate(flops=0, bytes_accessed=1024, transcendentals=0),
        name="prep",
    )(owner_of, unique_q, unique_kv, block)

    blocks = [block]
    ahead = behind = block
    recv = None
    for step in range(chips // 2 - 1):
        ahead, behind = along(ahead, 1), along(behind, -1)
        blocks += [ahead, behind]
        if step == chips // 2 - 2:
            send, ahead, behind = lax.optimization_barrier((send, ahead, behind))
            recv = lax.all_to_all(send, "branch", split_axis=0, concat_axis=0, tiled=True)
    upper = jnp.concatenate([ahead[:kv_heads], ahead[2 * kv_heads :]], axis=0)
    halves = [along(upper, 1), along(behind[kv_heads : 2 * kv_heads], -1)]
    blocks = blocks + [across(x) for x in blocks]
    me = jnp.full((1,), lax.axis_index("branch"), jnp.int32)
    prompt = prompt_k.shape[1]
    whole, split = len(blocks), 2
    early = prompt + whole * live
    late = split * live + CAP * branches
    rows = CAP * branches * GRP
    keys, values, bias = pl.pallas_call(
        functools.partial(gather_kernel, whole, branches),
        out_shape=(
            pltpu.VMEM((kv_heads, early, HD), jnp.bfloat16),
            pltpu.HBM((kv_heads, early, HD), jnp.bfloat16),
            pltpu.VMEM((8, early), jnp.float32),
        ),
        in_specs=[SMEM, SMEM] + [ANY] * (2 + whole),
        out_specs=(VMEM, ANY, VMEM),
        scratch_shapes=[
            pltpu.VMEM((kv_heads, early, HD), jnp.bfloat16),
            pltpu.VMEM((whole, live, HD), jnp.bfloat16),
            pltpu.SemaphoreType.DMA((3 * whole + 2 * kv_heads + 1,)),
        ],
        compiler_params=grant(16),
        cost_estimate=pl.CostEstimate(flops=0, bytes_accessed=8 * prompt_k.size, transcendentals=0),
        name="gather",
    )(me, prompt_mask, *[pltpu.with_memory_space_constraint(x, pltpu.HBM) for x in (prompt_k, prompt_v, *blocks)])
    halves, keys = lax.optimization_barrier((halves, keys))
    halves = halves + [across(x) for x in halves]
    outputs = pl.pallas_call(
        functools.partial(attend_kernel, split),
        out_shape=bf16(branches, CAP * heads, HD),
        in_specs=[SMEM, VMEM, VMEM] + [ANY] * (2 + 2 * split),
        out_specs=VMEM,
        scratch_shapes=[
            pltpu.VMEM((kv_heads, late, HD), jnp.bfloat16),
            pltpu.VMEM((kv_heads, late, HD), jnp.bfloat16),
            pltpu.VMEM((min(branches, 16) * TILE, early + late), jnp.float32),
            pltpu.VMEM((min(branches, 16) * TILE, early + late), jnp.float32),
            pltpu.VMEM((kv_heads, early, HD), jnp.bfloat16),
            pltpu.VMEM(recv.shape, jnp.bfloat16),
            *[pltpu.VMEM(x.shape, jnp.bfloat16) for x in halves],
            pltpu.SemaphoreType.DMA((1 + 2 * split + kv_heads,)),
        ],
        compiler_params=grant(40),
        cost_estimate=pl.CostEstimate(
            flops=4 * kv_heads * rows * HD * (early + late),
            bytes_accessed=4 * prompt_k.size,
            transcendentals=kv_heads * rows * (early + late),
        ),
        name="attend",
    )(me, keys, bias, *[pltpu.with_memory_space_constraint(x, pltpu.HBM) for x in (values, recv, *halves)])
    back = lax.all_to_all(outputs, "branch", split_axis=0, concat_axis=0, tiled=True)
    return pl.pallas_call(
        post_kernel,
        out_shape=jax.ShapeDtypeStruct((row_count, q_width), jnp.bfloat16),
        in_specs=[SMEM, VMEM],
        out_specs=VMEM,
        scratch_shapes=[
            pltpu.SMEM((branches,), jnp.int32),
            pltpu.VMEM((row_count, heads, HD), jnp.float32),
        ],
        compiler_params=grant(8),
        name="post",
    )(owner_of, back)


def solution(mesh):
    split = ("groups", "branch")
    in_specs = (
        P(split, None, None),
        P(split, None, None),
        P(split, None),
        P(split, None, None),
        P(split),
        P(split, None),
        P(split, None),
        P(split, None),
        P(split, None),
    )
    return jax.shard_map(body, mesh=mesh, in_specs=in_specs, out_specs=P(split, None), check_vma=False)
```

```python
import functools
import math

import jax
import jax.numpy as jnp
from jax import lax
from jax.experimental import pallas as pl
from jax.experimental.pallas import tpu as pltpu
from jax.sharding import PartitionSpec as P

HD = 128
GRP = 8
CAP = 2
TILE = 16
NONE = -1e30
ABSENT = 512.0
VMEM = pl.BlockSpec(memory_space=pltpu.VMEM)
SMEM = pl.BlockSpec(memory_space=pltpu.SMEM)
ANY = pl.BlockSpec(memory_space=pl.ANY)


def grant(mebibytes):
    return pltpu.CompilerParams(vmem_limit_bytes=mebibytes << 20)


def payload_kernel(pick_hbm, len_hbm, shared_hbm, out_ref, pick_ref, len_ref, shared_ref, sems):
    results, rows, width = shared_ref.shape
    branches = pick_ref.shape[1]
    moves = [
        pltpu.make_async_copy(source, target, sems.at[n])
        for n, (source, target) in enumerate(
            ((shared_hbm, shared_ref), (pick_hbm, pick_ref), (len_hbm, len_ref))
        )
    ]
    for move in moves:
        move.start()
    for move in moves:
        move.wait()
    live = results * rows
    lane = lax.broadcasted_iota(jnp.int32, (TILE, HD), 1)
    meta = jnp.zeros((TILE, HD), jnp.int32)
    for b in range(branches):
        meta = jnp.where(lane == b, pick_ref[0, b], meta)
    for r in range(results):
        meta = jnp.where(lane == branches + r, len_ref[0, r], meta)
    slabs = width // HD
    middle = slabs // 2 * live
    out_ref[middle : middle + TILE, :] = meta.astype(jnp.float32).astype(jnp.bfloat16)
    for j in range(slabs):
        part = shared_ref[:, :, j * HD : (j + 1) * HD].astype(jnp.float32)
        at = j * live + (TILE if 2 * j >= slabs else 0)
        out_ref[at : at + live, :] = part.reshape(live, HD).astype(jnp.bfloat16)


def place_rows(owner_ref, index_ref, count_ref):
    branches = count_ref.shape[0]
    for b in range(branches):
        count_ref[b] = 0
    for i in range(owner_ref.shape[0]):
        b = owner_ref[i]
        rank = count_ref[b]
        if index_ref is not None:
            index_ref[b * CAP + rank] = i
        count_ref[b] = rank + 1


def prep_kernel(owner_ref, q_hbm, kv_hbm, after_hbm, out_ref, index_ref, count_ref, q_ref, kv_ref, q3_ref, kv3_ref, sems):
    del after_hbm
    rows, q_width = q_ref.shape
    branches = out_ref.shape[0]
    heads = q_width // HD
    kv_heads = heads // GRP
    moves = [
        pltpu.make_async_copy(q_hbm, q_ref, sems.at[0]),
        pltpu.make_async_copy(kv_hbm, kv_ref, sems.at[1]),
    ]
    for move in moves:
        move.start()
    for b in range(branches * CAP):
        index_ref[b] = 0
    place_rows(owner_ref, index_ref, count_ref)
    for move in moves:
        move.wait()
    q3_ref[...] = q_ref[...].astype(jnp.float32).reshape(rows, heads, HD)
    kv3_ref[...] = kv_ref[...].astype(jnp.float32).reshape(rows, 2 * kv_heads, HD)

    @pl.loop(0, branches)
    def _(b):
        index = [index_ref[b * CAP + c] for c in range(CAP)]
        parts = [q3_ref[i].reshape(kv_heads, 1, GRP, HD) for i in index]
        tiles = jnp.concatenate(parts, axis=1).reshape(heads * CAP, HD)
        pairs = [kv3_ref[i] for i in index]
        there = [count_ref[b] > c for c in range(CAP)]
        keys = [jnp.where(t, p[:kv_heads], ABSENT) for t, p in zip(there, pairs)]
        values = [jnp.where(t, p[kv_heads:], 0.0) for t, p in zip(there, pairs)]
        out_ref[b] = jnp.concatenate([tiles] + keys + values, axis=0).astype(jnp.bfloat16)


def dot_nt(a, b):
    return lax.dot_general(a, b, (((1,), (1,)), ((), ())), preferred_element_type=jnp.float32)


FACTOR = math.log2(math.e) / math.sqrt(HD)


def starter(sems):
    free = iter(range(sems.shape[0]))

    def start(source, target):
        copy = pltpu.make_async_copy(source, target, sems.at[next(free)])
        copy.start()
        return copy

    return start


def picked(meta, me, branches):
    lane = lax.broadcasted_iota(jnp.int32, (1, HD), 1)
    meta = meta.astype(jnp.float32)[0:1, :]
    pick = jnp.sum(jnp.where(lane == me, meta, 0.0)).astype(jnp.int32)
    length = jnp.sum(jnp.where(lane == branches + pick, meta, 0.0)).astype(jnp.int32)
    return pick, jnp.where(pick < 0, 0, length)


def rows_picked(slab, pick):
    both = slab.astype(jnp.float32)
    rows = slab.shape[0] // 2
    return jnp.where(pick == 0, both[0:rows], both[rows:])


def gather_kernel(whole, split, me_ref, mask_ref, pk_hbm, pv_hbm, *refs):
    sources = refs[:whole]
    key_ref, value_hbm, bias_ref, value_ref, taken_ref, *blocks, sems = refs[whole:]
    slabs, room, _ = taken_ref.shape
    kv_heads = slabs // 2
    prompt = pk_hbm.shape[1]
    live = (blocks[0].shape[0] - TILE) // slabs
    rows = live // 2
    branches = whole + split
    middle = kv_heads * live
    start = starter(sems)
    moves = [start(source, target) for source, target in zip(sources, blocks)]
    wide = []
    for g in range(kv_heads):
        lanes = pl.ds(g * HD, HD)
        wide.append(start(pv_hbm.at[0, :, lanes], value_ref.at[g, pl.ds(0, prompt), :]))
        wide.append(start(pk_hbm.at[0, :, lanes], key_ref.at[g, pl.ds(0, prompt), :]))
    column = lax.broadcasted_iota(jnp.int32, (1, room), 1)
    seen = jnp.zeros((1, room), jnp.bool_)
    taken_ref[...] = jnp.zeros(taken_ref.shape, jnp.float32)
    for copy in moves:
        copy.wait()
    slot = jnp.int32(0)
    for block in blocks:
        pick, length = picked(block[middle : middle + TILE, :], me_ref[0], branches)
        at = pl.multiple_of(jnp.minimum(slot * rows, room - rows), 8)
        place = column - at
        seen = seen | ((place >= 0) & (place < length))

        @pl.when(pick >= 0)
        def _(block=block, pick=pick, at=at):
            for j in range(slabs):
                base = j * live + (TILE if j >= kv_heads else 0)
                taken_ref[j, pl.ds(at, rows), :] = rows_picked(block[base : base + live, :], pick)

        slot = slot + (pick >= 0).astype(jnp.int32)
    for g in range(kv_heads):
        key_ref[g, prompt : prompt + room, :] = taken_ref[g].astype(jnp.bfloat16)
        value_ref[g, prompt : prompt + room, :] = taken_ref[kv_heads + g].astype(jnp.bfloat16)
    blocks_seen = mask_ref.shape[1]
    biases = [
        jnp.full((1, prompt // blocks_seen), jnp.where(mask_ref[0, j] > 0, 0.0, NONE))
        for j in range(blocks_seen)
    ]
    bias = jnp.concatenate(biases + [jnp.where(seen, 0.0, NONE)], axis=1)
    bias_ref[...] = bias
    for copy in wide:
        copy.wait()
    leaving = start(value_ref, value_hbm)
    leaving.wait()


def attend_kernel(split, me_ref, key_ref, bias_ref, recv_ref, value_hbm, *refs):
    out_ref, late_key_ref, late_value_ref, first_ref, second_ref, value_ref, *halves, sems = refs[2 * split :]
    kv_heads, early, _ = key_ref.shape
    start = starter(sems)
    half_moves = [start(source, target) for source, target in zip(refs[: 2 * split], halves)]
    value_moves = [start(value_hbm.at[g], value_ref.at[g]) for g in range(kv_heads)]
    branches = recv_ref.shape[0]
    heads = kv_heads * GRP
    width = branches * CAP
    late = late_key_ref.shape[1]
    live = halves[1].shape[0] // kv_heads
    far = live // 2
    tail = late - width - split * far
    main = early - tail
    chunk = min(branches, 16)
    count = chunk * TILE

    def score(g, base, target):
        queries = recv_ref[pl.ds(base, chunk), g * TILE : (g + 1) * TILE, :].reshape(count, HD)
        target[:, 0:main] = dot_nt(queries, key_ref[g, 0:main, :]) + bias_ref[0:1, 0:main]

    if branches == chunk:
        score(0, 0, first_ref)
    for copy in half_moves:
        copy.wait()
    size = branches * TILE
    place = lax.broadcasted_iota(jnp.int32, (size, size), 1)
    wanted = lax.broadcasted_iota(jnp.int32, (size, size), 0)
    choose = jnp.where(place == lax.rem(wanted, width) * kv_heads + wanted // width, 1.0, 0.0).astype(jnp.bfloat16)
    unique = []
    for which in range(2):
        first = heads * CAP + which * TILE
        rows = recv_ref[:, first : first + TILE, :].reshape(size, HD)
        unique.append(jnp.dot(choose, rows, preferred_element_type=jnp.float32).reshape(kv_heads, width, HD))
    for copy in value_moves:
        copy.wait()
    choices = [picked(halves[2 * n][kv_heads * live :, :], me_ref[0], branches) for n in range(split)]
    for which, source, target in ((0, key_ref, late_key_ref), (1, value_ref, late_value_ref)):
        for g in range(kv_heads):
            rows = [rows_picked(halves[2 * n + which][g * live : (g + 1) * live, :], choices[n][0]) for n in range(split)]
            if tail:
                rows = [source[g, main:early, :].astype(jnp.float32)] + rows
            target[g] = jnp.concatenate(rows + [unique[which][g]], axis=0).astype(jnp.bfloat16)
    one = jnp.where(lax.broadcasted_iota(jnp.int32, (TILE, HD), 1) == 0, 1.0, 0.0).astype(jnp.bfloat16)
    absent = dot_nt(one, late_key_ref[0])[0:1, :] > ABSENT / 2
    spot = lax.broadcasted_iota(jnp.int32, (1, far), 1)
    late_bias = [jnp.where(spot < length, 0.0, NONE) for _, length in choices]
    if tail:
        late_bias = [bias_ref[0:1, main:early]] + late_bias
    late_bias = jnp.concatenate(late_bias + [jnp.zeros((1, width), jnp.float32)], axis=1)
    column = lax.broadcasted_iota(jnp.int32, (count, late), 1) - (late - width)
    own_slot = lax.broadcasted_iota(jnp.int32, (count, late), 0) // GRP

    def run(base):
        late_hidden = jnp.where((column >= 0) & (absent | (column > own_slot + base * CAP)), NONE, late_bias)

        def score_late(g, target):
            queries = recv_ref[pl.ds(base, chunk), g * TILE : (g + 1) * TILE, :].reshape(count, HD)
            target[:, main : main + late] = dot_nt(queries, late_key_ref[g]) + late_hidden

        def finish(g, source):
            scores = source[...]
            largest = jnp.max(scores, axis=1, keepdims=True)
            weights = jnp.exp2((scores - largest) * FACTOR)
            total = jnp.sum(weights, axis=1, keepdims=True)
            probs = weights.astype(jnp.bfloat16)
            mixed = jnp.dot(probs[:, 0:main], value_ref[g, 0:main, :], preferred_element_type=jnp.float32)
            mixed = mixed + jnp.dot(probs[:, main:], late_value_ref[g], preferred_element_type=jnp.float32)
            result = (mixed / total).astype(jnp.bfloat16)
            out_ref[pl.ds(base, chunk), g * TILE : (g + 1) * TILE, :] = result.reshape(chunk, TILE, HD)

        buffers = (first_ref, second_ref)
        if branches > chunk:
            score(0, base, buffers[0])
        score_late(0, buffers[0])
        for g in range(kv_heads):
            if g + 1 < kv_heads:
                score(g + 1, base, buffers[(g + 1) % 2])
                score_late(g + 1, buffers[(g + 1) % 2])
            finish(g, buffers[g % 2])

    if branches == chunk:
        run(0)
    else:
        @pl.loop(0, branches // chunk)
        def _(part):
            run(part * chunk)


def post_kernel(owner_ref, back_ref, out_ref, count_ref, o3_ref):
    rows, width = out_ref.shape
    heads = width // HD
    branches = back_ref.shape[0]
    for b in range(branches):
        count_ref[b] = 0

    @pl.loop(0, rows)
    def _(i):
        b = owner_ref[i]
        rank = count_ref[b]
        count_ref[b] = rank + 1
        tiles = back_ref[b].astype(jnp.float32).reshape(heads // GRP, CAP, GRP, HD)
        o3_ref[i] = jnp.where(rank == 0, tiles[:, 0], tiles[:, 1]).reshape(heads, HD)

    out_ref[...] = o3_ref[...].reshape(rows, width).astype(jnp.bfloat16)


def body(
    prompt_k, prompt_v, prompt_mask, shared_kv, shared_len, send_pick, unique_q, unique_kv, unique_owner
):
    branches = lax.axis_size("branch")
    chips = branches // 2
    row_count, q_width = unique_q.shape
    heads = q_width // HD
    kv_width = unique_kv.shape[1] // 2
    kv_heads = kv_width // HD
    results, result_rows, _ = shared_kv.shape
    owner_of = unique_owner[:, 0]
    live = results * result_rows
    slot_rows = CAP * heads + 2 * TILE

    def bf16(*shape):
        return jax.ShapeDtypeStruct(shape, jnp.bfloat16)

    block = pl.pallas_call(
        payload_kernel,
        out_shape=bf16(2 * kv_heads * live + TILE, HD),
        in_specs=[ANY] * 3,
        out_specs=VMEM,
        scratch_shapes=[
            pltpu.SMEM(send_pick.shape, jnp.int32),
            pltpu.SMEM((1, results), jnp.int32),
            pltpu.VMEM(shared_kv.shape, jnp.bfloat16),
            pltpu.SemaphoreType.DMA((3,)),
        ],
        compiler_params=grant(56),
        name="payload",
    )(send_pick, shared_len.reshape(1, results), shared_kv)

    order = list(range(0, chips, 2)) + list(range(1, chips, 2))[::-1]

    def along(x, step):
        pairs = [
            (order[p] * 2 + core, order[(p + step) % chips] * 2 + core)
            for p in range(chips)
            for core in range(2)
        ]
        return lax.ppermute(x, "branch", pairs)

    def across(x):
        return lax.ppermute(x, "branch", [(i, i ^ 1) for i in range(branches)])

    send = pl.pallas_call(
        prep_kernel,
        out_shape=bf16(branches, slot_rows, HD),
        in_specs=[SMEM, ANY, ANY, ANY],
        out_specs=VMEM,
        scratch_shapes=[
            pltpu.SMEM((branches * CAP,), jnp.int32),
            pltpu.SMEM((branches,), jnp.int32),
            pltpu.VMEM(unique_q.shape, jnp.bfloat16),
            pltpu.VMEM(unique_kv.shape, jnp.bfloat16),
            pltpu.VMEM((row_count, heads, HD), jnp.float32),
            pltpu.VMEM((row_count, 2 * kv_heads, HD), jnp.float32),
            pltpu.SemaphoreType.DMA((2,)),
        ],
        compiler_params=grant(56),
        cost_estimate=pl.CostEstimate(flops=0, bytes_accessed=1024, transcendentals=0),
        name="prep",
    )(owner_of, unique_q, unique_kv, block)

    blocks = [block]
    ahead = behind = block
    for step in range(chips // 2 - 1):
        ahead, behind = along(ahead, 1), along(behind, -1)
        blocks += [ahead, behind]
        if step == 0:
            send, ahead = lax.optimization_barrier((send, ahead))
    send, ahead, behind = lax.optimization_barrier((send, ahead, behind))
    recv = lax.all_to_all(send, "branch", split_axis=0, concat_axis=0, tiled=True)
    cut = kv_heads * live + TILE
    halves = [along(ahead[:cut], 1), along(behind[cut:], -1)]
    blocks = blocks + [across(x) for x in blocks]
    me = jnp.full((1,), lax.axis_index("branch"), jnp.int32)
    prompt = prompt_k.shape[1]
    whole, split = len(blocks), 2
    room = branches * 3 // 4 * result_rows
    early = prompt + room
    width = CAP * branches
    tail = early % HD
    chunk_rows = min(branches, 16) * TILE
    rows = width * GRP
    arrays = [pltpu.with_memory_space_constraint(x, pltpu.HBM) for x in (prompt_k, prompt_v, *blocks)]
    keys, values, bias = pl.pallas_call(
        functools.partial(gather_kernel, whole, split),
        out_shape=(
            pltpu.VMEM((kv_heads, early, HD), jnp.bfloat16),
            pltpu.HBM((kv_heads, early, HD), jnp.bfloat16),
            pltpu.VMEM((1, early), jnp.float32),
        ),
        in_specs=[SMEM, SMEM] + [ANY] * len(arrays),
        out_specs=(VMEM, ANY, VMEM),
        scratch_shapes=[
            pltpu.VMEM((kv_heads, early, HD), jnp.bfloat16),
            pltpu.VMEM((2 * kv_heads, room, HD), jnp.float32),
            *[pltpu.VMEM(x.shape, jnp.bfloat16) for x in arrays[2:]],
            pltpu.SemaphoreType.DMA((len(arrays) - 2 + 2 * kv_heads + 1,)),
        ],
        compiler_params=grant(40 if branches > 16 else 20),
        cost_estimate=pl.CostEstimate(flops=0, bytes_accessed=8 * prompt_k.size, transcendentals=0),
        name="gather",
    )(me, prompt_mask, *arrays)
    halves, keys = lax.optimization_barrier((halves, keys))
    halves = halves + [across(x) for x in halves]
    late = tail + split * result_rows + width
    outputs = pl.pallas_call(
        functools.partial(attend_kernel, split),
        out_shape=bf16(branches, CAP * heads, HD),
        in_specs=[SMEM, VMEM, VMEM, VMEM] + [ANY] * (1 + 2 * split),
        out_specs=VMEM,
        scratch_shapes=[
            pltpu.VMEM((kv_heads, late, HD), jnp.bfloat16),
            pltpu.VMEM((kv_heads, late, HD), jnp.bfloat16),
            pltpu.VMEM((chunk_rows, early - tail + late), jnp.float32),
            pltpu.VMEM((chunk_rows, early - tail + late), jnp.float32),
            pltpu.VMEM((kv_heads, early, HD), jnp.bfloat16),
            *[pltpu.VMEM(x.shape, jnp.bfloat16) for x in halves],
            pltpu.SemaphoreType.DMA((2 * split + kv_heads,)),
        ],
        compiler_params=grant(40),
        cost_estimate=pl.CostEstimate(
            flops=4 * kv_heads * rows * HD * (early + width),
            bytes_accessed=4 * prompt_k.size,
            transcendentals=kv_heads * rows * (early + width),
        ),
        name="attend",
    )(me, keys, bias, recv, *[pltpu.with_memory_space_constraint(x, pltpu.HBM) for x in (values, *halves)])
    back = lax.all_to_all(outputs, "branch", split_axis=0, concat_axis=0, tiled=True)
    return pl.pallas_call(
        post_kernel,
        out_shape=jax.ShapeDtypeStruct((row_count, q_width), jnp.bfloat16),
        in_specs=[SMEM, VMEM],
        out_specs=VMEM,
        scratch_shapes=[
            pltpu.SMEM((branches,), jnp.int32),
            pltpu.VMEM((row_count, heads, HD), jnp.float32),
        ],
        compiler_params=grant(8),
        name="post",
    )(owner_of, back)


def solution(mesh):
    split = ("groups", "branch")
    in_specs = (
        P(split, None, None),
        P(split, None, None),
        P(split, None),
        P(split, None, None),
        P(split),
        P(split, None),
        P(split, None),
        P(split, None),
        P(split, None),
    )
    return jax.shard_map(body, mesh=mesh, in_specs=in_specs, out_specs=P(split, None), check_vma=False)
```

```python
import functools
import math

import jax
import jax.numpy as jnp
from jax import lax
from jax.experimental import pallas as pl
from jax.experimental.pallas import tpu as pltpu
from jax.sharding import PartitionSpec as P

HD = 128
GRP = 8
CAP = 2
TILE = 16
NONE = -1e30
ABSENT = 512.0
VMEM = pl.BlockSpec(memory_space=pltpu.VMEM)
SMEM = pl.BlockSpec(memory_space=pltpu.SMEM)
ANY = pl.BlockSpec(memory_space=pl.ANY)


def grant(mebibytes):
    return pltpu.CompilerParams(vmem_limit_bytes=mebibytes << 20)


def payload_kernel(pick_hbm, len_hbm, shared_hbm, out_ref, pick_ref, len_ref, shared_ref, sems):
    results, rows, width = shared_ref.shape
    branches = pick_ref.shape[1]
    moves = [
        pltpu.make_async_copy(source, target, sems.at[n])
        for n, (source, target) in enumerate(
            ((shared_hbm, shared_ref), (pick_hbm, pick_ref), (len_hbm, len_ref))
        )
    ]
    for move in moves:
        move.start()
    for move in moves:
        move.wait()
    live = results * rows
    lane = lax.broadcasted_iota(jnp.int32, (TILE, HD), 1)
    meta = jnp.zeros((TILE, HD), jnp.int32)
    for b in range(branches):
        meta = jnp.where(lane == b, pick_ref[0, b], meta)
    for r in range(results):
        meta = jnp.where(lane == branches + r, len_ref[0, r], meta)
    slabs = width // HD
    middle = slabs // 2 * live
    out_ref[middle : middle + TILE, :] = meta.astype(jnp.float32).astype(jnp.bfloat16)
    for j in range(slabs):
        part = shared_ref[:, :, j * HD : (j + 1) * HD].astype(jnp.float32)
        at = j * live + (TILE if 2 * j >= slabs else 0)
        out_ref[at : at + live, :] = part.reshape(live, HD).astype(jnp.bfloat16)


def place_rows(owner_ref, index_ref, count_ref):
    branches = count_ref.shape[0]
    for b in range(branches):
        count_ref[b] = 0
    for i in range(owner_ref.shape[0]):
        b = owner_ref[i]
        rank = count_ref[b]
        if index_ref is not None:
            index_ref[b * CAP + rank] = i
        count_ref[b] = rank + 1


def prep_kernel(owner_ref, q_hbm, kv_hbm, after_hbm, out_ref, index_ref, count_ref, q_ref, kv_ref, q3_ref, kv3_ref, sems):
    del after_hbm
    rows, q_width = q_ref.shape
    branches = out_ref.shape[0]
    heads = q_width // HD
    kv_heads = heads // GRP
    moves = [
        pltpu.make_async_copy(q_hbm, q_ref, sems.at[0]),
        pltpu.make_async_copy(kv_hbm, kv_ref, sems.at[1]),
    ]
    for move in moves:
        move.start()
    for b in range(branches * CAP):
        index_ref[b] = 0
    place_rows(owner_ref, index_ref, count_ref)
    for move in moves:
        move.wait()
    q3_ref[...] = q_ref[...].astype(jnp.float32).reshape(rows, heads, HD)
    kv3_ref[...] = kv_ref[...].astype(jnp.float32).reshape(rows, 2 * kv_heads, HD)

    @pl.loop(0, branches)
    def _(b):
        index = [index_ref[b * CAP + c] for c in range(CAP)]
        parts = [q3_ref[i].reshape(kv_heads, 1, GRP, HD) for i in index]
        tiles = jnp.concatenate(parts, axis=1).reshape(heads * CAP, HD)
        pairs = [kv3_ref[i] for i in index]
        there = [count_ref[b] > c for c in range(CAP)]
        keys = [jnp.where(t, p[:kv_heads], ABSENT) for t, p in zip(there, pairs)]
        values = [jnp.where(t, p[kv_heads:], 0.0) for t, p in zip(there, pairs)]
        out_ref[b] = jnp.concatenate([tiles] + keys + values, axis=0).astype(jnp.bfloat16)


def dot_nt(a, b):
    return lax.dot_general(a, b, (((1,), (1,)), ((), ())), preferred_element_type=jnp.float32)


FACTOR = math.log2(math.e) / math.sqrt(HD)


def starter(sems):
    free = iter(range(sems.shape[0]))

    def start(source, target):
        copy = pltpu.make_async_copy(source, target, sems.at[next(free)])
        copy.start()
        return copy

    return start


def picked(meta, me, branches):
    lane = lax.broadcasted_iota(jnp.int32, (1, HD), 1)
    meta = meta.astype(jnp.float32)[0:1, :]
    pick = jnp.sum(jnp.where(lane == me, meta, 0.0)).astype(jnp.int32)
    length = jnp.sum(jnp.where(lane == branches + pick, meta, 0.0)).astype(jnp.int32)
    return pick, jnp.where(pick < 0, 0, length)


def rows_picked(slab, pick):
    both = slab.astype(jnp.float32)
    rows = slab.shape[0] // 2
    return jnp.where(pick == 0, both[0:rows], both[rows:])


def gather_kernel(whole, split, me_ref, mask_ref, pk_hbm, pv_hbm, *refs):
    sources = refs[:whole]
    near_key, near_value, bias_ref, far_key_hbm, far_value_hbm = refs[whole : whole + 5]
    far_key, far_value, taken_ref, *blocks, sems = refs[whole + 5 :]
    near = near_key.shape[0]
    slabs, room, _ = taken_ref.shape
    kv_heads = slabs // 2
    prompt = pk_hbm.shape[1]
    live = (blocks[0].shape[0] - TILE) // slabs
    rows = live // 2
    branches = whole + split
    middle = kv_heads * live
    start = starter(sems)
    moves = [start(source, target) for source, target in zip(sources, blocks)]
    wide = []
    homes = [(near_key.at[g], near_value.at[g]) for g in range(near)]
    homes += [(far_key.at[g], far_value.at[g]) for g in range(kv_heads - near)]
    for g, (key_ref, value_ref) in enumerate(homes):
        lanes = pl.ds(g * HD, HD)
        wide.append(start(pv_hbm.at[0, :, lanes], value_ref.at[pl.ds(0, prompt), :]))
        wide.append(start(pk_hbm.at[0, :, lanes], key_ref.at[pl.ds(0, prompt), :]))
    column = lax.broadcasted_iota(jnp.int32, (1, room), 1)
    seen = jnp.zeros((1, room), jnp.bool_)
    taken_ref[...] = jnp.zeros(taken_ref.shape, jnp.float32)
    for copy in moves:
        copy.wait()
    slot = jnp.int32(0)
    for block in blocks:
        pick, length = picked(block[middle : middle + TILE, :], me_ref[0], branches)
        at = pl.multiple_of(jnp.minimum(slot * rows, room - rows), 8)
        place = column - at
        seen = seen | ((place >= 0) & (place < length))

        @pl.when(pick >= 0)
        def _(block=block, pick=pick, at=at):
            for j in range(slabs):
                base = j * live + (TILE if j >= kv_heads else 0)
                taken_ref[j, pl.ds(at, rows), :] = rows_picked(block[base : base + live, :], pick)

        slot = slot + (pick >= 0).astype(jnp.int32)
    for g, (key_ref, value_ref) in enumerate(homes):
        key_ref[prompt : prompt + room, :] = taken_ref[g].astype(jnp.bfloat16)
        value_ref[prompt : prompt + room, :] = taken_ref[kv_heads + g].astype(jnp.bfloat16)
    blocks_seen = mask_ref.shape[1]
    biases = [
        jnp.full((1, prompt // blocks_seen), jnp.where(mask_ref[0, j] > 0, 0.0, NONE))
        for j in range(blocks_seen)
    ]
    bias = jnp.concatenate(biases + [jnp.where(seen, 0.0, NONE)], axis=1)
    bias_ref[...] = bias
    for copy in wide:
        copy.wait()
    leaving = [start(far_key, far_key_hbm), start(far_value, far_value_hbm)]
    for copy in leaving:
        copy.wait()


def attend_kernel(split, me_ref, near_key, near_value, bias_ref, recv_ref, *refs):
    halves = refs[: 2 * split]
    far_key_hbm, far_value_hbm, out_ref, late_key_ref, late_value_ref, first_ref, second_ref, far_key, far_value, sems = (
        refs[2 * split :]
    )
    near, early, _ = near_key.shape
    kv_heads = near + far_key.shape[0]
    early_of = [(near_key.at[g], near_value.at[g]) for g in range(near)]
    early_of += [(far_key.at[g], far_value.at[g]) for g in range(kv_heads - near)]
    start = starter(sems)
    far_moves = [start(far_key_hbm, far_key), start(far_value_hbm, far_value)]
    branches = recv_ref.shape[0]
    heads = kv_heads * GRP
    width = branches * CAP
    late = late_key_ref.shape[1]
    live = halves[1].shape[0] // kv_heads
    far = live // 2
    tail = late - width - split * far
    main = early - tail
    chunk = min(branches, 16)
    count = chunk * TILE

    def score(g, base, target):
        queries = recv_ref[pl.ds(base, chunk), g * TILE : (g + 1) * TILE, :].reshape(count, HD)
        target[:, 0:main] = dot_nt(queries, early_of[g][0][0:main, :]) + bias_ref[0:1, 0:main]

    if branches == chunk:
        score(0, 0, first_ref)
        score(1, 0, second_ref)
    size = branches * TILE
    place = lax.broadcasted_iota(jnp.int32, (size, size), 1)
    wanted = lax.broadcasted_iota(jnp.int32, (size, size), 0)
    choose = jnp.where(place == lax.rem(wanted, width) * kv_heads + wanted // width, 1.0, 0.0).astype(jnp.bfloat16)
    unique = []
    for which in range(2):
        first = heads * CAP + which * TILE
        rows = recv_ref[:, first : first + TILE, :].reshape(size, HD)
        unique.append(jnp.dot(choose, rows, preferred_element_type=jnp.float32).reshape(kv_heads, width, HD))
    choices = [picked(halves[2 * n][kv_heads * live :, :], me_ref[0], branches) for n in range(split)]

    def fill(g):
        for which, target in ((0, late_key_ref), (1, late_value_ref)):
            rows = [rows_picked(halves[2 * n + which][g * live : (g + 1) * live, :], choices[n][0]) for n in range(split)]
            if tail:
                rows = [early_of[g][which][main:early, :].astype(jnp.float32)] + rows
            target[g] = jnp.concatenate(rows + [unique[which][g]], axis=0).astype(jnp.bfloat16)

    for g in range(near):
        fill(g)
    one = jnp.where(lax.broadcasted_iota(jnp.int32, (TILE, HD), 1) == 0, 1.0, 0.0).astype(jnp.bfloat16)
    absent = dot_nt(one, late_key_ref[0])[0:1, :] > ABSENT / 2
    spot = lax.broadcasted_iota(jnp.int32, (1, far), 1)
    late_bias = [jnp.where(spot < length, 0.0, NONE) for _, length in choices]
    if tail:
        late_bias = [bias_ref[0:1, main:early]] + late_bias
    late_bias = jnp.concatenate(late_bias + [jnp.zeros((1, width), jnp.float32)], axis=1)
    column = lax.broadcasted_iota(jnp.int32, (count, late), 1) - (late - width)
    own_slot = lax.broadcasted_iota(jnp.int32, (count, late), 0) // GRP

    def far_part():
        for copy in far_moves:
            copy.wait()
        for g in range(near, kv_heads):
            fill(g)

    if branches > chunk:
        far_part()

    def run(base):
        late_hidden = jnp.where((column >= 0) & (absent | (column > own_slot + base * CAP)), NONE, late_bias)

        def score_late(g, target):
            queries = recv_ref[pl.ds(base, chunk), g * TILE : (g + 1) * TILE, :].reshape(count, HD)
            target[:, main : main + late] = dot_nt(queries, late_key_ref[g]) + late_hidden

        def finish(g, source):
            scores = source[...]
            largest = jnp.max(scores, axis=1, keepdims=True)
            weights = jnp.exp2((scores - largest) * FACTOR)
            total = jnp.sum(weights, axis=1, keepdims=True)
            probs = weights.astype(jnp.bfloat16)
            mixed = jnp.dot(probs[:, 0:main], early_of[g][1][0:main, :], preferred_element_type=jnp.float32)
            mixed = mixed + jnp.dot(probs[:, main:], late_value_ref[g], preferred_element_type=jnp.float32)
            result = (mixed / total).astype(jnp.bfloat16)
            out_ref[pl.ds(base, chunk), g * TILE : (g + 1) * TILE, :] = result.reshape(chunk, TILE, HD)

        buffers = (first_ref, second_ref)
        if branches > chunk:
            score(0, base, buffers[0])
            score(1, base, buffers[1])
        score_late(0, buffers[0])
        score_late(1, buffers[1])
        for g in range(kv_heads):
            finish(g, buffers[g % 2])
            if g + 2 == near and branches == chunk:
                far_part()
            if g + 2 < kv_heads:
                score(g + 2, base, buffers[g % 2])
                score_late(g + 2, buffers[g % 2])

    if branches == chunk:
        run(0)
    else:
        @pl.loop(0, branches // chunk)
        def _(part):
            run(part * chunk)


def post_kernel(owner_ref, back_ref, out_ref, count_ref, o3_ref):
    rows, width = out_ref.shape
    heads = width // HD
    branches = back_ref.shape[0]
    for b in range(branches):
        count_ref[b] = 0

    @pl.loop(0, rows)
    def _(i):
        b = owner_ref[i]
        rank = count_ref[b]
        count_ref[b] = rank + 1
        tiles = back_ref[b].astype(jnp.float32).reshape(heads // GRP, CAP, GRP, HD)
        o3_ref[i] = jnp.where(rank == 0, tiles[:, 0], tiles[:, 1]).reshape(heads, HD)

    out_ref[...] = o3_ref[...].reshape(rows, width).astype(jnp.bfloat16)


def body(
    prompt_k, prompt_v, prompt_mask, shared_kv, shared_len, send_pick, unique_q, unique_kv, unique_owner
):
    branches = lax.axis_size("branch")
    chips = branches // 2
    row_count, q_width = unique_q.shape
    heads = q_width // HD
    kv_width = unique_kv.shape[1] // 2
    kv_heads = kv_width // HD
    results, result_rows, _ = shared_kv.shape
    owner_of = unique_owner[:, 0]
    live = results * result_rows
    slot_rows = CAP * heads + 2 * TILE

    def bf16(*shape):
        return jax.ShapeDtypeStruct(shape, jnp.bfloat16)

    block = pl.pallas_call(
        payload_kernel,
        out_shape=bf16(2 * kv_heads * live + TILE, HD),
        in_specs=[ANY] * 3,
        out_specs=VMEM,
        scratch_shapes=[
            pltpu.SMEM(send_pick.shape, jnp.int32),
            pltpu.SMEM((1, results), jnp.int32),
            pltpu.VMEM(shared_kv.shape, jnp.bfloat16),
            pltpu.SemaphoreType.DMA((3,)),
        ],
        compiler_params=grant(56),
        name="payload",
    )(send_pick, shared_len.reshape(1, results), shared_kv)

    order = list(range(0, chips, 2)) + list(range(1, chips, 2))[::-1]

    def along(x, step):
        pairs = [
            (order[p] * 2 + core, order[(p + step) % chips] * 2 + core)
            for p in range(chips)
            for core in range(2)
        ]
        return lax.ppermute(x, "branch", pairs)

    def across(x):
        return lax.ppermute(x, "branch", [(i, i ^ 1) for i in range(branches)])

    send = pl.pallas_call(
        prep_kernel,
        out_shape=bf16(branches, slot_rows, HD),
        in_specs=[SMEM, ANY, ANY, ANY],
        out_specs=VMEM,
        scratch_shapes=[
            pltpu.SMEM((branches * CAP,), jnp.int32),
            pltpu.SMEM((branches,), jnp.int32),
            pltpu.VMEM(unique_q.shape, jnp.bfloat16),
            pltpu.VMEM(unique_kv.shape, jnp.bfloat16),
            pltpu.VMEM((row_count, heads, HD), jnp.float32),
            pltpu.VMEM((row_count, 2 * kv_heads, HD), jnp.float32),
            pltpu.SemaphoreType.DMA((2,)),
        ],
        compiler_params=grant(56),
        cost_estimate=pl.CostEstimate(flops=0, bytes_accessed=1024, transcendentals=0),
        name="prep",
    )(owner_of, unique_q, unique_kv, block)

    blocks = [block]
    ahead = behind = block
    for step in range(chips // 2 - 1):
        ahead, behind = along(ahead, 1), along(behind, -1)
        blocks += [ahead, behind]
        if step == 0:
            send, ahead = lax.optimization_barrier((send, ahead))
    send, ahead, behind = lax.optimization_barrier((send, ahead, behind))
    recv = lax.all_to_all(send, "branch", split_axis=0, concat_axis=0, tiled=True)
    cut = kv_heads * live + TILE
    halves = [along(ahead[:cut], 1), along(behind[cut:], -1)]
    blocks = blocks + [across(x) for x in blocks]
    me = jnp.full((1,), lax.axis_index("branch"), jnp.int32)
    prompt = prompt_k.shape[1]
    whole, split = len(blocks), 2
    room = branches * 3 // 4 * result_rows
    early = prompt + room
    width = CAP * branches
    tail = early % HD
    chunk_rows = min(branches, 16) * TILE
    rows = width * GRP
    arrays = [pltpu.with_memory_space_constraint(x, pltpu.HBM) for x in (prompt_k, prompt_v, *blocks)]
    near = kv_heads // 2 - 1
    keys, values, bias, *far_early = pl.pallas_call(
        functools.partial(gather_kernel, whole, split),
        out_shape=(
            pltpu.VMEM((near, early, HD), jnp.bfloat16),
            pltpu.VMEM((near, early, HD), jnp.bfloat16),
            pltpu.VMEM((1, early), jnp.float32),
            pltpu.HBM((kv_heads - near, early, HD), jnp.bfloat16),
            pltpu.HBM((kv_heads - near, early, HD), jnp.bfloat16),
        ),
        in_specs=[SMEM, SMEM] + [ANY] * len(arrays),
        out_specs=(VMEM, VMEM, VMEM, ANY, ANY),
        scratch_shapes=[
            pltpu.VMEM((kv_heads - near, early, HD), jnp.bfloat16),
            pltpu.VMEM((kv_heads - near, early, HD), jnp.bfloat16),
            pltpu.VMEM((2 * kv_heads, room, HD), jnp.float32),
            *[pltpu.VMEM(x.shape, jnp.bfloat16) for x in arrays[2:]],
            pltpu.SemaphoreType.DMA((len(arrays) - 2 + 2 * kv_heads + 2,)),
        ],
        compiler_params=grant(40 if branches > 16 else 20),
        cost_estimate=pl.CostEstimate(flops=0, bytes_accessed=8 * prompt_k.size, transcendentals=0),
        name="gather",
    )(me, prompt_mask, *arrays)
    halves, keys, values = lax.optimization_barrier((halves, keys, values))
    halves = halves + [across(x) for x in halves]
    late = tail + split * result_rows + width
    outputs = pl.pallas_call(
        functools.partial(attend_kernel, split),
        out_shape=bf16(branches, CAP * heads, HD),
        in_specs=[SMEM] + [VMEM] * (4 + 2 * split) + [ANY] * 2,
        out_specs=VMEM,
        scratch_shapes=[
            pltpu.VMEM((kv_heads, late, HD), jnp.bfloat16),
            pltpu.VMEM((kv_heads, late, HD), jnp.bfloat16),
            pltpu.VMEM((chunk_rows, early - tail + late), jnp.float32),
            pltpu.VMEM((chunk_rows, early - tail + late), jnp.float32),
            pltpu.VMEM((kv_heads - near, early, HD), jnp.bfloat16),
            pltpu.VMEM((kv_heads - near, early, HD), jnp.bfloat16),
            pltpu.SemaphoreType.DMA((2,)),
        ],
        compiler_params=grant(40),
        cost_estimate=pl.CostEstimate(
            flops=4 * kv_heads * rows * HD * (early + width),
            bytes_accessed=4 * prompt_k.size,
            transcendentals=kv_heads * rows * (early + width),
        ),
        name="attend",
    )(me, keys, values, bias, recv, *halves, *[pltpu.with_memory_space_constraint(x, pltpu.HBM) for x in far_early])
    back = lax.all_to_all(outputs, "branch", split_axis=0, concat_axis=0, tiled=True)
    return pl.pallas_call(
        post_kernel,
        out_shape=jax.ShapeDtypeStruct((row_count, q_width), jnp.bfloat16),
        in_specs=[SMEM, VMEM],
        out_specs=VMEM,
        scratch_shapes=[
            pltpu.SMEM((branches,), jnp.int32),
            pltpu.VMEM((row_count, heads, HD), jnp.float32),
        ],
        compiler_params=grant(8),
        name="post",
    )(owner_of, back)


def solution(mesh):
    split = ("groups", "branch")
    in_specs = (
        P(split, None, None),
        P(split, None, None),
        P(split, None),
        P(split, None, None),
        P(split),
        P(split, None),
        P(split, None),
        P(split, None),
        P(split, None),
    )
    return jax.shard_map(body, mesh=mesh, in_specs=in_specs, out_specs=P(split, None), check_vma=False)
```

```python
import functools
import math

import jax
import jax.numpy as jnp
from jax import lax
from jax.experimental import pallas as pl
from jax.experimental.pallas import tpu as pltpu
from jax.sharding import PartitionSpec as P

HD = 128
GRP = 8
CAP = 2
TILE = 16
NONE = -1e30
ABSENT = 512.0
VMEM = pl.BlockSpec(memory_space=pltpu.VMEM)
SMEM = pl.BlockSpec(memory_space=pltpu.SMEM)
ANY = pl.BlockSpec(memory_space=pl.ANY)


def grant(mebibytes):
    return pltpu.CompilerParams(vmem_limit_bytes=mebibytes << 20)


def payload_kernel(pick_hbm, len_hbm, shared_hbm, out_ref, pick_ref, len_ref, shared_ref, sems):
    results, rows, width = shared_ref.shape
    branches = pick_ref.shape[1]
    moves = [
        pltpu.make_async_copy(source, target, sems.at[n])
        for n, (source, target) in enumerate(
            ((shared_hbm, shared_ref), (pick_hbm, pick_ref), (len_hbm, len_ref))
        )
    ]
    for move in moves:
        move.start()
    for move in moves:
        move.wait()
    live = results * rows
    lane = lax.broadcasted_iota(jnp.int32, (TILE, HD), 1)
    meta = jnp.zeros((TILE, HD), jnp.int32)
    for b in range(branches):
        meta = jnp.where(lane == b, pick_ref[0, b], meta)
    for r in range(results):
        meta = jnp.where(lane == branches + r, len_ref[0, r], meta)
    slabs = width // HD
    middle = slabs // 2 * live
    out_ref[middle : middle + TILE, :] = meta.astype(jnp.float32).astype(jnp.bfloat16)
    for j in range(slabs):
        part = shared_ref[:, :, j * HD : (j + 1) * HD].astype(jnp.float32)
        at = j * live + (TILE if 2 * j >= slabs else 0)
        out_ref[at : at + live, :] = part.reshape(live, HD).astype(jnp.bfloat16)


def place_rows(owner_ref, index_ref, count_ref):
    branches = count_ref.shape[0]
    for b in range(branches):
        count_ref[b] = 0
    for i in range(owner_ref.shape[0]):
        b = owner_ref[i]
        rank = count_ref[b]
        if index_ref is not None:
            index_ref[b * CAP + rank] = i
        count_ref[b] = rank + 1


def ring_place(me, chips):
    chip = me // 2
    return jnp.where(lax.rem(chip, 2) == 0, chip // 2, chips - 1 - chip // 2)


def has_short_way(me, chips):
    if chips != 8:
        return jnp.bool_(False)
    place = lax.rem(ring_place(me, chips), 4)
    return (place == 1) | (place == 2)


def prep_kernel(owner_ref, q_hbm, kv_hbm, after_hbm, out_ref, index_ref, count_ref, q_ref, kv_ref, q3_ref, kv3_ref, sems):
    del after_hbm
    rows, q_width = q_ref.shape
    branches = out_ref.shape[0]
    heads = q_width // HD
    kv_heads = heads // GRP
    moves = [
        pltpu.make_async_copy(q_hbm, q_ref, sems.at[0]),
        pltpu.make_async_copy(kv_hbm, kv_ref, sems.at[1]),
    ]
    for move in moves:
        move.start()
    for b in range(branches * CAP):
        index_ref[b] = 0
    place_rows(owner_ref, index_ref, count_ref)
    for move in moves:
        move.wait()
    q3_ref[...] = q_ref[...].astype(jnp.float32).reshape(rows, heads, HD)
    kv3_ref[...] = kv_ref[...].astype(jnp.float32).reshape(rows, 2 * kv_heads, HD)

    @pl.loop(0, branches)
    def _(b):
        index = [index_ref[b * CAP + c] for c in range(CAP)]
        parts = [q3_ref[i].reshape(kv_heads, 1, GRP, HD) for i in index]
        tiles = jnp.concatenate(parts, axis=1).reshape(heads * CAP, HD)
        pairs = [kv3_ref[i] for i in index]
        there = [count_ref[b] > c for c in range(CAP)]
        keys = [jnp.where(t, p[:kv_heads], ABSENT) for t, p in zip(there, pairs)]
        values = [jnp.where(t, p[kv_heads:], 0.0) for t, p in zip(there, pairs)]
        out_ref[b] = jnp.concatenate([tiles] + keys + values, axis=0).astype(jnp.bfloat16)


def dot_nt(a, b):
    return lax.dot_general(a, b, (((1,), (1,)), ((), ())), preferred_element_type=jnp.float32)


FACTOR = math.log2(math.e) / math.sqrt(HD)


def starter(sems):
    free = iter(range(sems.shape[0]))

    def start(source, target):
        copy = pltpu.make_async_copy(source, target, sems.at[next(free)])
        copy.start()
        return copy

    return start


def picked(meta, me, branches):
    lane = lax.broadcasted_iota(jnp.int32, (1, HD), 1)
    meta = meta.astype(jnp.float32)[0:1, :]
    pick = jnp.sum(jnp.where(lane == me, meta, 0.0)).astype(jnp.int32)
    length = jnp.sum(jnp.where(lane == branches + pick, meta, 0.0)).astype(jnp.int32)
    return pick, jnp.where(pick < 0, 0, length)


def rows_picked(slab, pick):
    both = slab.astype(jnp.float32)
    rows = slab.shape[0] // 2
    return jnp.where(pick == 0, both[0:rows], both[rows:])


def gather_kernel(whole, branches, short, me_ref, mask_ref, pk_hbm, pv_hbm, *refs):
    sources = refs[:whole]
    near_key, near_value, bias_ref, far_key_hbm, far_value_hbm = refs[whole : whole + 5]
    far_key, far_value, taken_ref, *blocks, sems = refs[whole + 5 :]
    near = near_key.shape[0]
    slabs, room, _ = taken_ref.shape
    kv_heads = slabs // 2
    prompt = pk_hbm.shape[1]
    live = (blocks[0].shape[0] - TILE) // slabs
    rows = live // 2
    middle = kv_heads * live
    start = starter(sems)
    moves = [start(source, target) for source, target in zip(sources, blocks)]
    wide = []
    homes = [(near_key.at[g], near_value.at[g]) for g in range(near)]
    homes += [(far_key.at[g], far_value.at[g]) for g in range(kv_heads - near)]
    for g, (key_ref, value_ref) in enumerate(homes):
        lanes = pl.ds(g * HD, HD)
        wide.append(start(pv_hbm.at[0, :, lanes], value_ref.at[pl.ds(0, prompt), :]))
        wide.append(start(pk_hbm.at[0, :, lanes], key_ref.at[pl.ds(0, prompt), :]))
    column = lax.broadcasted_iota(jnp.int32, (1, room), 1)
    seen = jnp.zeros((1, room), jnp.bool_)
    taken_ref[...] = jnp.zeros(taken_ref.shape, jnp.float32)
    for copy in moves:
        copy.wait()
    slot = jnp.int32(0)
    straight = has_short_way(me_ref[0], branches // 2)
    for n, block in enumerate(blocks):
        pick, length = picked(block[middle : middle + TILE, :], me_ref[0], branches)
        if n >= whole - short:
            pick, length = jnp.where(straight, pick, -1), jnp.where(straight, length, 0)
        at = pl.multiple_of(jnp.minimum(slot * rows, room - rows), 8)
        place = column - at
        seen = seen | ((place >= 0) & (place < length))

        @pl.when(pick >= 0)
        def _(block=block, pick=pick, at=at):
            for j in range(slabs):
                base = j * live + (TILE if j >= kv_heads else 0)
                taken_ref[j, pl.ds(at, rows), :] = rows_picked(block[base : base + live, :], pick)

        slot = slot + (pick >= 0).astype(jnp.int32)
    for g, (key_ref, value_ref) in enumerate(homes):
        key_ref[prompt : prompt + room, :] = taken_ref[g].astype(jnp.bfloat16)
        value_ref[prompt : prompt + room, :] = taken_ref[kv_heads + g].astype(jnp.bfloat16)
    blocks_seen = mask_ref.shape[1]
    biases = [
        jnp.full((1, prompt // blocks_seen), jnp.where(mask_ref[0, j] > 0, 0.0, NONE))
        for j in range(blocks_seen)
    ]
    bias = jnp.concatenate(biases + [jnp.where(seen, 0.0, NONE)], axis=1)
    bias_ref[...] = bias
    for copy in wide:
        copy.wait()
    leaving = [start(far_key, far_key_hbm), start(far_value, far_value_hbm)]
    for copy in leaving:
        copy.wait()


def attend_kernel(split, me_ref, near_key, near_value, bias_ref, recv_ref, *refs):
    halves = refs[:split]
    far_key_hbm, far_value_hbm, out_ref, late_key_ref, late_value_ref, first_ref, second_ref, far_key, far_value, sems = (
        refs[split:]
    )
    near, early, _ = near_key.shape
    kv_heads = near + far_key.shape[0]
    early_of = [(near_key.at[g], near_value.at[g]) for g in range(near)]
    early_of += [(far_key.at[g], far_value.at[g]) for g in range(kv_heads - near)]
    start = starter(sems)
    far_moves = [start(far_key_hbm, far_key), start(far_value_hbm, far_value)]
    branches = recv_ref.shape[0]
    heads = kv_heads * GRP
    width = branches * CAP
    late = late_key_ref.shape[1]
    live = (halves[0].shape[0] - TILE) // (2 * kv_heads)
    middle = kv_heads * live
    far = live // 2
    tail = late - width - split * far
    main = early - tail
    chunk = min(branches, 16)
    count = chunk * TILE

    def score(g, base, target):
        queries = recv_ref[pl.ds(base, chunk), g * TILE : (g + 1) * TILE, :].reshape(count, HD)
        target[:, 0:main] = dot_nt(queries, early_of[g][0][0:main, :]) + bias_ref[0:1, 0:main]

    if branches == chunk:
        score(0, 0, first_ref)
        score(1, 0, second_ref)
    size = branches * TILE
    place = lax.broadcasted_iota(jnp.int32, (size, size), 1)
    wanted = lax.broadcasted_iota(jnp.int32, (size, size), 0)
    choose = jnp.where(place == lax.rem(wanted, width) * kv_heads + wanted // width, 1.0, 0.0).astype(jnp.bfloat16)
    unique = []
    for which in range(2):
        first = heads * CAP + which * TILE
        rows = recv_ref[:, first : first + TILE, :].reshape(size, HD)
        unique.append(jnp.dot(choose, rows, preferred_element_type=jnp.float32).reshape(kv_heads, width, HD))
    choices = [picked(halves[n][middle : middle + TILE, :], me_ref[0], branches) for n in range(split)]
    straight = has_short_way(me_ref[0], branches // 2)
    choices = [(pick, jnp.where(straight, 0, length)) for pick, length in choices]

    def fill(g):
        for which, target in ((0, late_key_ref), (1, late_value_ref)):
            at = which * (middle + TILE) + g * live
            rows = [rows_picked(halves[n][at : at + live, :], choices[n][0]) for n in range(split)]
            if tail:
                rows = [early_of[g][which][main:early, :].astype(jnp.float32)] + rows
            target[g] = jnp.concatenate(rows + [unique[which][g]], axis=0).astype(jnp.bfloat16)

    for g in range(near):
        fill(g)
    one = jnp.where(lax.broadcasted_iota(jnp.int32, (TILE, HD), 1) == 0, 1.0, 0.0).astype(jnp.bfloat16)
    absent = dot_nt(one, late_key_ref[0])[0:1, :] > ABSENT / 2
    spot = lax.broadcasted_iota(jnp.int32, (1, far), 1)
    late_bias = [jnp.where(spot < length, 0.0, NONE) for _, length in choices]
    if tail:
        late_bias = [bias_ref[0:1, main:early]] + late_bias
    late_bias = jnp.concatenate(late_bias + [jnp.zeros((1, width), jnp.float32)], axis=1)
    column = lax.broadcasted_iota(jnp.int32, (count, late), 1) - (late - width)
    own_slot = lax.broadcasted_iota(jnp.int32, (count, late), 0) // GRP

    def far_part():
        for copy in far_moves:
            copy.wait()
        for g in range(near, kv_heads):
            fill(g)

    if branches > chunk:
        far_part()

    def run(base):
        late_hidden = jnp.where((column >= 0) & (absent | (column > own_slot + base * CAP)), NONE, late_bias)

        def score_late(g, target):
            queries = recv_ref[pl.ds(base, chunk), g * TILE : (g + 1) * TILE, :].reshape(count, HD)
            target[:, main : main + late] = dot_nt(queries, late_key_ref[g]) + late_hidden

        def finish(g, source):
            scores = source[...]
            largest = jnp.max(scores, axis=1, keepdims=True)
            weights = jnp.exp2((scores - largest) * FACTOR)
            total = jnp.sum(weights, axis=1, keepdims=True)
            probs = weights.astype(jnp.bfloat16)
            mixed = jnp.dot(probs[:, 0:main], early_of[g][1][0:main, :], preferred_element_type=jnp.float32)
            mixed = mixed + jnp.dot(probs[:, main:], late_value_ref[g], preferred_element_type=jnp.float32)
            result = (mixed / total).astype(jnp.bfloat16)
            out_ref[pl.ds(base, chunk), g * TILE : (g + 1) * TILE, :] = result.reshape(chunk, TILE, HD)

        buffers = (first_ref, second_ref)
        if branches > chunk:
            score(0, base, buffers[0])
            score(1, base, buffers[1])
        score_late(0, buffers[0])
        score_late(1, buffers[1])
        for g in range(kv_heads):
            finish(g, buffers[g % 2])
            if g + 2 == near and branches == chunk:
                far_part()
            if g + 2 < kv_heads:
                score(g + 2, base, buffers[g % 2])
                score_late(g + 2, buffers[g % 2])

    if branches == chunk:
        run(0)
    else:
        @pl.loop(0, branches // chunk)
        def _(part):
            run(part * chunk)


def post_kernel(owner_ref, back_ref, out_ref, count_ref, o3_ref):
    rows, width = out_ref.shape
    heads = width // HD
    branches = back_ref.shape[0]
    for b in range(branches):
        count_ref[b] = 0

    @pl.loop(0, rows)
    def _(i):
        b = owner_ref[i]
        rank = count_ref[b]
        count_ref[b] = rank + 1
        tiles = back_ref[b].astype(jnp.float32).reshape(heads // GRP, CAP, GRP, HD)
        o3_ref[i] = jnp.where(rank == 0, tiles[:, 0], tiles[:, 1]).reshape(heads, HD)

    out_ref[...] = o3_ref[...].reshape(rows, width).astype(jnp.bfloat16)


def body(
    prompt_k, prompt_v, prompt_mask, shared_kv, shared_len, send_pick, unique_q, unique_kv, unique_owner
):
    branches = lax.axis_size("branch")
    chips = branches // 2
    row_count, q_width = unique_q.shape
    heads = q_width // HD
    kv_width = unique_kv.shape[1] // 2
    kv_heads = kv_width // HD
    results, result_rows, _ = shared_kv.shape
    owner_of = unique_owner[:, 0]
    live = results * result_rows
    slot_rows = CAP * heads + 2 * TILE

    def bf16(*shape):
        return jax.ShapeDtypeStruct(shape, jnp.bfloat16)

    block = pl.pallas_call(
        payload_kernel,
        out_shape=bf16(2 * kv_heads * live + TILE, HD),
        in_specs=[ANY] * 3,
        out_specs=VMEM,
        scratch_shapes=[
            pltpu.SMEM(send_pick.shape, jnp.int32),
            pltpu.SMEM((1, results), jnp.int32),
            pltpu.VMEM(shared_kv.shape, jnp.bfloat16),
            pltpu.SemaphoreType.DMA((3,)),
        ],
        compiler_params=grant(56),
        name="payload",
    )(send_pick, shared_len.reshape(1, results), shared_kv)

    order = list(range(0, chips, 2)) + list(range(1, chips, 2))[::-1]

    def hop(x, places):
        pairs = [(order[p] * 2 + core, order[q] * 2 + core) for p, q in places for core in range(2)]
        return lax.ppermute(x, "branch", pairs)

    def along(x, step):
        return hop(x, [(p, (p + step) % chips) for p in range(chips)])

    def across(x):
        return lax.ppermute(x, "branch", [(i, i ^ 1) for i in range(branches)])

    send = pl.pallas_call(
        prep_kernel,
        out_shape=bf16(branches, slot_rows, HD),
        in_specs=[SMEM, ANY, ANY, ANY],
        out_specs=VMEM,
        scratch_shapes=[
            pltpu.SMEM((branches * CAP,), jnp.int32),
            pltpu.SMEM((branches,), jnp.int32),
            pltpu.VMEM(unique_q.shape, jnp.bfloat16),
            pltpu.VMEM(unique_kv.shape, jnp.bfloat16),
            pltpu.VMEM((row_count, heads, HD), jnp.float32),
            pltpu.VMEM((row_count, 2 * kv_heads, HD), jnp.float32),
            pltpu.SemaphoreType.DMA((2,)),
        ],
        compiler_params=grant(56),
        cost_estimate=pl.CostEstimate(flops=0, bytes_accessed=1024, transcendentals=0),
        name="prep",
    )(owner_of, unique_q, unique_kv, block)

    me = jnp.full((1,), lax.axis_index("branch"), jnp.int32)
    blocks, shorts = [block], []
    ahead = behind = block
    for step in range(chips // 2 - 1):
        ahead, behind = along(ahead, 1), along(behind, -1)
        blocks += [ahead, behind]
        if step == 0:
            send, ahead = lax.optimization_barrier((send, ahead))
        if step == 0 and chips == 8:
            place = lax.rem(ring_place(me[0], chips), 4)
            facing = jnp.where(place == 2, ahead, behind)
            shorts = [hop(facing, [(1, 6), (6, 1), (2, 5), (5, 2)])]
    send, ahead, behind, *shorts = lax.optimization_barrier((send, ahead, behind, *shorts))
    recv = lax.all_to_all(send, "branch", split_axis=0, concat_axis=0, tiled=True)
    if shorts:
        last = jnp.where(lax.rem(ring_place(me[0], chips), 4) == 0, behind, ahead)
        halves = [hop(last, [(7, 0), (0, 7), (3, 4), (4, 3)])]
    else:
        halves = [along(ahead, 1)]
    shorts = shorts + [across(x) for x in shorts]
    blocks = blocks + [across(x) for x in blocks] + shorts
    prompt = prompt_k.shape[1]
    whole, split = len(blocks), 2
    room = branches * 3 // 4 * result_rows
    early = prompt + room
    width = CAP * branches
    tail = early % HD
    chunk_rows = min(branches, 16) * TILE
    rows = width * GRP
    arrays = [pltpu.with_memory_space_constraint(x, pltpu.HBM) for x in (prompt_k, prompt_v, *blocks)]
    near = kv_heads // 2 - 1
    keys, values, bias, *far_early = pl.pallas_call(
        functools.partial(gather_kernel, whole, branches, len(shorts)),
        out_shape=(
            pltpu.VMEM((near, early, HD), jnp.bfloat16),
            pltpu.VMEM((near, early, HD), jnp.bfloat16),
            pltpu.VMEM((1, early), jnp.float32),
            pltpu.HBM((kv_heads - near, early, HD), jnp.bfloat16),
            pltpu.HBM((kv_heads - near, early, HD), jnp.bfloat16),
        ),
        in_specs=[SMEM, SMEM] + [ANY] * len(arrays),
        out_specs=(VMEM, VMEM, VMEM, ANY, ANY),
        scratch_shapes=[
            pltpu.VMEM((kv_heads - near, early, HD), jnp.bfloat16),
            pltpu.VMEM((kv_heads - near, early, HD), jnp.bfloat16),
            pltpu.VMEM((2 * kv_heads, room, HD), jnp.float32),
            *[pltpu.VMEM(x.shape, jnp.bfloat16) for x in arrays[2:]],
            pltpu.SemaphoreType.DMA((len(arrays) - 2 + 2 * kv_heads + 2,)),
        ],
        compiler_params=grant(40 if branches > 16 else 20),
        cost_estimate=pl.CostEstimate(flops=0, bytes_accessed=8 * prompt_k.size, transcendentals=0),
        name="gather",
    )(me, prompt_mask, *arrays)
    halves, keys, values = lax.optimization_barrier((halves, keys, values))
    halves = halves + [across(x) for x in halves]
    late = tail + split * result_rows + width
    outputs = pl.pallas_call(
        functools.partial(attend_kernel, split),
        out_shape=bf16(branches, CAP * heads, HD),
        in_specs=[SMEM] + [VMEM] * (4 + split) + [ANY] * 2,
        out_specs=VMEM,
        scratch_shapes=[
            pltpu.VMEM((kv_heads, late, HD), jnp.bfloat16),
            pltpu.VMEM((kv_heads, late, HD), jnp.bfloat16),
            pltpu.VMEM((chunk_rows, early - tail + late), jnp.float32),
            pltpu.VMEM((chunk_rows, early - tail + late), jnp.float32),
            pltpu.VMEM((kv_heads - near, early, HD), jnp.bfloat16),
            pltpu.VMEM((kv_heads - near, early, HD), jnp.bfloat16),
            pltpu.SemaphoreType.DMA((2,)),
        ],
        compiler_params=grant(40),
        cost_estimate=pl.CostEstimate(
            flops=4 * kv_heads * rows * HD * (early + width),
            bytes_accessed=4 * prompt_k.size,
            transcendentals=kv_heads * rows * (early + width),
        ),
        name="attend",
    )(me, keys, values, bias, recv, *halves, *[pltpu.with_memory_space_constraint(x, pltpu.HBM) for x in far_early])
    back = lax.all_to_all(outputs, "branch", split_axis=0, concat_axis=0, tiled=True)
    return pl.pallas_call(
        post_kernel,
        out_shape=jax.ShapeDtypeStruct((row_count, q_width), jnp.bfloat16),
        in_specs=[SMEM, VMEM],
        out_specs=VMEM,
        scratch_shapes=[
            pltpu.SMEM((branches,), jnp.int32),
            pltpu.VMEM((row_count, heads, HD), jnp.float32),
        ],
        compiler_params=grant(8),
        name="post",
    )(owner_of, back)


def solution(mesh):
    split = ("groups", "branch")
    in_specs = (
        P(split, None, None),
        P(split, None, None),
        P(split, None),
        P(split, None, None),
        P(split),
        P(split, None),
        P(split, None),
        P(split, None),
        P(split, None),
    )
    return jax.shard_map(body, mesh=mesh, in_specs=in_specs, out_specs=P(split, None), check_vma=False)
```

```python
import functools
import math

import jax
import jax.numpy as jnp
from jax import lax
from jax.experimental import pallas as pl
from jax.experimental.pallas import tpu as pltpu
from jax.sharding import PartitionSpec as P

HD = 128
GRP = 8
CAP = 2
TILE = 16
NONE = -1e30
ABSENT = 512.0
VMEM = pl.BlockSpec(memory_space=pltpu.VMEM)
SMEM = pl.BlockSpec(memory_space=pltpu.SMEM)
ANY = pl.BlockSpec(memory_space=pl.ANY)


def grant(mebibytes):
    return pltpu.CompilerParams(vmem_limit_bytes=mebibytes << 20)


def payload_kernel(pick_hbm, len_hbm, shared_hbm, out_ref, pick_ref, len_ref, shared_ref, sems):
    results, rows, width = shared_ref.shape
    branches = pick_ref.shape[1]
    moves = [
        pltpu.make_async_copy(source, target, sems.at[n])
        for n, (source, target) in enumerate(
            ((shared_hbm, shared_ref), (pick_hbm, pick_ref), (len_hbm, len_ref))
        )
    ]
    for move in moves:
        move.start()
    for move in moves:
        move.wait()
    live = results * rows
    lane = lax.broadcasted_iota(jnp.int32, (TILE, HD), 1)
    meta = jnp.zeros((TILE, HD), jnp.int32)
    for b in range(branches):
        meta = jnp.where(lane == b, pick_ref[0, b], meta)
    for r in range(results):
        meta = jnp.where(lane == branches + r, len_ref[0, r], meta)
    slabs = width // HD
    middle = slabs // 2 * live
    out_ref[middle : middle + TILE, :] = meta.astype(jnp.float32).astype(jnp.bfloat16)
    for j in range(slabs):
        part = shared_ref[:, :, j * HD : (j + 1) * HD].astype(jnp.float32)
        at = j * live + (TILE if 2 * j >= slabs else 0)
        out_ref[at : at + live, :] = part.reshape(live, HD).astype(jnp.bfloat16)


def place_rows(owner_ref, index_ref, count_ref):
    branches = count_ref.shape[0]
    for b in range(branches):
        count_ref[b] = 0
    for i in range(owner_ref.shape[0]):
        b = owner_ref[i]
        rank = count_ref[b]
        if index_ref is not None:
            index_ref[b * CAP + rank] = i
        count_ref[b] = rank + 1


def ring_place(me, chips):
    chip = me // 2
    return jnp.where(lax.rem(chip, 2) == 0, chip // 2, chips - 1 - chip // 2)


def has_short_way(me, chips):
    if chips != 8:
        return jnp.bool_(False)
    place = lax.rem(ring_place(me, chips), 4)
    return (place == 1) | (place == 2)


def prep_kernel(owner_ref, q_hbm, kv_hbm, after_hbm, out_ref, index_ref, count_ref, q_ref, kv_ref, q3_ref, kv3_ref, sems):
    del after_hbm
    rows, q_width = q_ref.shape
    branches = out_ref.shape[0]
    heads = q_width // HD
    kv_heads = heads // GRP
    moves = [
        pltpu.make_async_copy(q_hbm, q_ref, sems.at[0]),
        pltpu.make_async_copy(kv_hbm, kv_ref, sems.at[1]),
    ]
    for move in moves:
        move.start()
    for b in range(branches * CAP):
        index_ref[b] = 0
    place_rows(owner_ref, index_ref, count_ref)
    for move in moves:
        move.wait()
    q3_ref[...] = q_ref[...].astype(jnp.float32).reshape(rows, heads, HD)
    kv3_ref[...] = kv_ref[...].astype(jnp.float32).reshape(rows, 2 * kv_heads, HD)

    @pl.loop(0, branches)
    def _(b):
        index = [index_ref[b * CAP + c] for c in range(CAP)]
        parts = [q3_ref[i].reshape(kv_heads, 1, GRP, HD) for i in index]
        tiles = jnp.concatenate(parts, axis=1).reshape(heads * CAP, HD)
        pairs = [kv3_ref[i] for i in index]
        there = [count_ref[b] > c for c in range(CAP)]
        keys = [jnp.where(t, p[:kv_heads], ABSENT) for t, p in zip(there, pairs)]
        values = [jnp.where(t, p[kv_heads:], 0.0) for t, p in zip(there, pairs)]
        out_ref[b] = jnp.concatenate([tiles] + keys + values, axis=0).astype(jnp.bfloat16)


def dot_nt(a, b):
    return lax.dot_general(a, b, (((1,), (1,)), ((), ())), preferred_element_type=jnp.float32)


FACTOR = math.log2(math.e) / math.sqrt(HD)


def starter(sems):
    free = iter(range(sems.shape[0]))

    def start(source, target):
        copy = pltpu.make_async_copy(source, target, sems.at[next(free)])
        copy.start()
        return copy

    return start


def picked(meta, me, branches):
    lane = lax.broadcasted_iota(jnp.int32, (1, HD), 1)
    meta = meta.astype(jnp.float32)[0:1, :]
    pick = jnp.sum(jnp.where(lane == me, meta, 0.0)).astype(jnp.int32)
    length = jnp.sum(jnp.where(lane == branches + pick, meta, 0.0)).astype(jnp.int32)
    return pick, jnp.where(pick < 0, 0, length)


def rows_picked(slab, pick):
    both = slab.astype(jnp.float32)
    rows = slab.shape[0] // 2
    return jnp.where(pick == 0, both[0:rows], both[rows:])


def gather_kernel(whole, branches, short, me_ref, mask_ref, pk_hbm, pv_hbm, *refs):
    sources = refs[:whole]
    near_key, near_value, bias_ref, far_key_hbm, far_value_hbm = refs[whole : whole + 5]
    far_key, far_value, taken_ref, *blocks, sems = refs[whole + 5 :]
    near = near_key.shape[0]
    slabs, room, _ = taken_ref.shape
    kv_heads = slabs // 2
    prompt = pk_hbm.shape[1]
    live = (blocks[0].shape[0] - TILE) // slabs
    rows = live // 2
    middle = kv_heads * live
    start = starter(sems)
    moves = [start(source, target) for source, target in zip(sources, blocks)]
    wide = []
    homes = [(near_key.at[g], near_value.at[g]) for g in range(near)]
    homes += [(far_key.at[g], far_value.at[g]) for g in range(kv_heads - near)]
    for g, (key_ref, value_ref) in enumerate(homes):
        lanes = pl.ds(g * HD, HD)
        wide.append(start(pv_hbm.at[0, :, lanes], value_ref.at[pl.ds(0, prompt), :]))
        wide.append(start(pk_hbm.at[0, :, lanes], key_ref.at[pl.ds(0, prompt), :]))
    column = lax.broadcasted_iota(jnp.int32, (1, room), 1)
    seen = jnp.zeros((1, room), jnp.bool_)
    taken_ref[...] = jnp.zeros(taken_ref.shape, jnp.float32)
    for copy in moves:
        copy.wait()
    slot = jnp.int32(0)
    straight = has_short_way(me_ref[0], branches // 2)
    early = pl.ds(0, prompt)
    late = pl.ds(prompt, room)
    leaving = []
    for n, block in enumerate(blocks):
        if n == len(blocks) // 2:
            for copy in wide:
                copy.wait()
            leaving += [
                start(far_key.at[:, early, :], far_key_hbm.at[:, early, :]),
                start(far_value.at[:, early, :], far_value_hbm.at[:, early, :]),
            ]
        pick, length = picked(block[middle : middle + TILE, :], me_ref[0], branches)
        if n >= whole - short:
            pick, length = jnp.where(straight, pick, -1), jnp.where(straight, length, 0)
        at = pl.multiple_of(jnp.minimum(slot * rows, room - rows), 8)
        place = column - at
        seen = seen | ((place >= 0) & (place < length))

        @pl.when(pick >= 0)
        def _(block=block, pick=pick, at=at):
            for j in range(slabs):
                base = j * live + (TILE if j >= kv_heads else 0)
                taken_ref[j, pl.ds(at, rows), :] = rows_picked(block[base : base + live, :], pick)

        slot = slot + (pick >= 0).astype(jnp.int32)
    for g, (key_ref, value_ref) in enumerate(homes):
        key_ref[prompt : prompt + room, :] = taken_ref[g].astype(jnp.bfloat16)
        value_ref[prompt : prompt + room, :] = taken_ref[kv_heads + g].astype(jnp.bfloat16)
    leaving += [
        start(far_key.at[:, late, :], far_key_hbm.at[:, late, :]),
        start(far_value.at[:, late, :], far_value_hbm.at[:, late, :]),
    ]
    blocks_seen = mask_ref.shape[1]
    biases = [
        jnp.full((1, prompt // blocks_seen), jnp.where(mask_ref[0, j] > 0, 0.0, NONE))
        for j in range(blocks_seen)
    ]
    bias = jnp.concatenate(biases + [jnp.where(seen, 0.0, NONE)], axis=1)
    bias_ref[...] = bias
    for copy in leaving:
        copy.wait()


def attend_kernel(split, me_ref, near_key, near_value, bias_ref, recv_ref, *refs):
    halves = refs[: 2 * split]
    far_key_hbm, far_value_hbm, out_ref, late_key_ref, late_value_ref, first_ref, second_ref, far_key, far_value, sems = (
        refs[2 * split :]
    )
    near, early, _ = near_key.shape
    kv_heads = near + far_key.shape[0]
    early_of = [(near_key.at[g], near_value.at[g]) for g in range(near)]
    early_of += [(far_key.at[g], far_value.at[g]) for g in range(kv_heads - near)]
    start = starter(sems)
    far_moves = [start(far_key_hbm, far_key), start(far_value_hbm, far_value)]
    branches = recv_ref.shape[0]
    heads = kv_heads * GRP
    width = branches * CAP
    late = late_key_ref.shape[1]
    live = halves[1].shape[0] // kv_heads
    far = live // 2
    tail = late - width - split * far
    main = early - tail
    chunk = min(branches, 16)
    count = chunk * TILE

    def score(g, base, target):
        queries = recv_ref[pl.ds(base, chunk), g * TILE : (g + 1) * TILE, :].reshape(count, HD)
        target[:, 0:main] = dot_nt(queries, early_of[g][0][0:main, :]) + bias_ref[0:1, 0:main]

    if branches == chunk:
        score(0, 0, first_ref)
        score(1, 0, second_ref)
    size = branches * TILE
    place = lax.broadcasted_iota(jnp.int32, (size, size), 1)
    wanted = lax.broadcasted_iota(jnp.int32, (size, size), 0)
    choose = jnp.where(place == lax.rem(wanted, width) * kv_heads + wanted // width, 1.0, 0.0).astype(jnp.bfloat16)
    unique = []
    for which in range(2):
        first = heads * CAP + which * TILE
        rows = recv_ref[:, first : first + TILE, :].reshape(size, HD)
        unique.append(jnp.dot(choose, rows, preferred_element_type=jnp.float32).reshape(kv_heads, width, HD))
    choices = [picked(halves[2 * n][kv_heads * live :, :], me_ref[0], branches) for n in range(split)]
    straight = has_short_way(me_ref[0], branches // 2)
    choices = [(pick, jnp.where(straight, 0, length)) for pick, length in choices]

    def fill(g):
        for which, target in ((0, late_key_ref), (1, late_value_ref)):
            rows = [rows_picked(halves[2 * n + which][g * live : (g + 1) * live, :], choices[n][0]) for n in range(split)]
            if tail:
                rows = [early_of[g][which][main:early, :].astype(jnp.float32)] + rows
            target[g] = jnp.concatenate(rows + [unique[which][g]], axis=0).astype(jnp.bfloat16)

    for g in range(near):
        fill(g)
    one = jnp.where(lax.broadcasted_iota(jnp.int32, (TILE, HD), 1) == 0, 1.0, 0.0).astype(jnp.bfloat16)
    absent = dot_nt(one, late_key_ref[0])[0:1, :] > ABSENT / 2
    spot = lax.broadcasted_iota(jnp.int32, (1, far), 1)
    late_bias = [jnp.where(spot < length, 0.0, NONE) for _, length in choices]
    if tail:
        late_bias = [bias_ref[0:1, main:early]] + late_bias
    late_bias = jnp.concatenate(late_bias + [jnp.zeros((1, width), jnp.float32)], axis=1)
    column = lax.broadcasted_iota(jnp.int32, (count, late), 1) - (late - width)
    own_slot = lax.broadcasted_iota(jnp.int32, (count, late), 0) // GRP

    def far_part():
        for copy in far_moves:
            copy.wait()
        for g in range(near, kv_heads):
            fill(g)

    if branches > chunk:
        far_part()

    def run(base):
        late_hidden = jnp.where((column >= 0) & (absent | (column > own_slot + base * CAP)), NONE, late_bias)

        def score_late(g, target):
            queries = recv_ref[pl.ds(base, chunk), g * TILE : (g + 1) * TILE, :].reshape(count, HD)
            target[:, main : main + late] = dot_nt(queries, late_key_ref[g]) + late_hidden

        def finish(g, source):
            scores = source[...]
            largest = jnp.max(scores, axis=1, keepdims=True)
            weights = jnp.exp2((scores - largest) * FACTOR)
            total = jnp.sum(weights, axis=1, keepdims=True)
            probs = weights.astype(jnp.bfloat16)
            mixed = jnp.dot(probs[:, 0:main], early_of[g][1][0:main, :], preferred_element_type=jnp.float32)
            mixed = mixed + jnp.dot(probs[:, main:], late_value_ref[g], preferred_element_type=jnp.float32)
            result = (mixed / total).astype(jnp.bfloat16)
            out_ref[pl.ds(base, chunk), g * TILE : (g + 1) * TILE, :] = result.reshape(chunk, TILE, HD)

        buffers = (first_ref, second_ref)
        if branches > chunk:
            score(0, base, buffers[0])
            score(1, base, buffers[1])
        score_late(0, buffers[0])
        score_late(1, buffers[1])
        for g in range(kv_heads):
            finish(g, buffers[g % 2])
            if g + 2 == near and branches == chunk:
                far_part()
            if g + 2 < kv_heads:
                score(g + 2, base, buffers[g % 2])
                score_late(g + 2, buffers[g % 2])

    if branches == chunk:
        run(0)
    else:
        @pl.loop(0, branches // chunk)
        def _(part):
            run(part * chunk)


def post_kernel(owner_ref, back_ref, out_ref, count_ref, o3_ref):
    rows, width = out_ref.shape
    heads = width // HD
    branches = back_ref.shape[0]
    for b in range(branches):
        count_ref[b] = 0

    @pl.loop(0, rows)
    def _(i):
        b = owner_ref[i]
        rank = count_ref[b]
        count_ref[b] = rank + 1
        tiles = back_ref[b].astype(jnp.float32).reshape(heads // GRP, CAP, GRP, HD)
        o3_ref[i] = jnp.where(rank == 0, tiles[:, 0], tiles[:, 1]).reshape(heads, HD)

    out_ref[...] = o3_ref[...].reshape(rows, width).astype(jnp.bfloat16)


def body(
    prompt_k, prompt_v, prompt_mask, shared_kv, shared_len, send_pick, unique_q, unique_kv, unique_owner
):
    branches = lax.axis_size("branch")
    chips = branches // 2
    row_count, q_width = unique_q.shape
    heads = q_width // HD
    kv_width = unique_kv.shape[1] // 2
    kv_heads = kv_width // HD
    results, result_rows, _ = shared_kv.shape
    owner_of = unique_owner[:, 0]
    live = results * result_rows
    slot_rows = CAP * heads + 2 * TILE

    def bf16(*shape):
        return jax.ShapeDtypeStruct(shape, jnp.bfloat16)

    block = pl.pallas_call(
        payload_kernel,
        out_shape=bf16(2 * kv_heads * live + TILE, HD),
        in_specs=[ANY] * 3,
        out_specs=VMEM,
        scratch_shapes=[
            pltpu.SMEM(send_pick.shape, jnp.int32),
            pltpu.SMEM((1, results), jnp.int32),
            pltpu.VMEM(shared_kv.shape, jnp.bfloat16),
            pltpu.SemaphoreType.DMA((3,)),
        ],
        compiler_params=grant(56),
        name="payload",
    )(send_pick, shared_len.reshape(1, results), shared_kv)

    order = list(range(0, chips, 2)) + list(range(1, chips, 2))[::-1]

    def hop(x, places):
        pairs = [(order[p] * 2 + core, order[q] * 2 + core) for p, q in places for core in range(2)]
        return lax.ppermute(x, "branch", pairs)

    def along(x, step):
        return hop(x, [(p, (p + step) % chips) for p in range(chips)])

    def across(x):
        return lax.ppermute(x, "branch", [(i, i ^ 1) for i in range(branches)])

    send = pl.pallas_call(
        prep_kernel,
        out_shape=bf16(branches, slot_rows, HD),
        in_specs=[SMEM, ANY, ANY, ANY],
        out_specs=VMEM,
        scratch_shapes=[
            pltpu.SMEM((branches * CAP,), jnp.int32),
            pltpu.SMEM((branches,), jnp.int32),
            pltpu.VMEM(unique_q.shape, jnp.bfloat16),
            pltpu.VMEM(unique_kv.shape, jnp.bfloat16),
            pltpu.VMEM((row_count, heads, HD), jnp.float32),
            pltpu.VMEM((row_count, 2 * kv_heads, HD), jnp.float32),
            pltpu.SemaphoreType.DMA((2,)),
        ],
        compiler_params=grant(56),
        cost_estimate=pl.CostEstimate(flops=0, bytes_accessed=1024, transcendentals=0),
        name="prep",
    )(owner_of, unique_q, unique_kv, block)

    me = jnp.full((1,), lax.axis_index("branch"), jnp.int32)
    blocks, shorts = [block], []
    ahead = behind = block
    for step in range(chips // 2 - 1):
        ahead, behind = along(ahead, 1), along(behind, -1)
        blocks += [ahead, behind]
        if step == 0:
            send, ahead = lax.optimization_barrier((send, ahead))
        if step == 0 and chips == 8:
            place = lax.rem(ring_place(me[0], chips), 4)
            facing = jnp.where(place == 2, ahead, behind)
            shorts = [hop(facing, [(1, 6), (6, 1), (2, 5), (5, 2)])]
    send, ahead, behind, *shorts = lax.optimization_barrier((send, ahead, behind, *shorts))
    recv = lax.all_to_all(send, "branch", split_axis=0, concat_axis=0, tiled=True)
    if shorts:
        last = jnp.where(lax.rem(ring_place(me[0], chips), 4) == 0, behind, ahead)
        halves = [hop(last, [(7, 0), (0, 7), (3, 4), (4, 3)])]
    else:
        halves = [along(ahead, 1)]
    shorts = shorts + [across(x) for x in shorts]
    blocks = blocks + [across(x) for x in blocks] + shorts
    prompt = prompt_k.shape[1]
    whole, split = len(blocks), 2
    room = branches * 3 // 4 * result_rows
    early = prompt + room
    width = CAP * branches
    tail = early % HD
    chunk_rows = min(branches, 16) * TILE
    rows = width * GRP
    arrays = [pltpu.with_memory_space_constraint(x, pltpu.HBM) for x in (prompt_k, prompt_v, *blocks)]
    near = kv_heads // 2 - 1
    keys, values, bias, *far_early = pl.pallas_call(
        functools.partial(gather_kernel, whole, branches, len(shorts)),
        out_shape=(
            pltpu.VMEM((near, early, HD), jnp.bfloat16),
            pltpu.VMEM((near, early, HD), jnp.bfloat16),
            pltpu.VMEM((1, early), jnp.float32),
            pltpu.HBM((kv_heads - near, early, HD), jnp.bfloat16),
            pltpu.HBM((kv_heads - near, early, HD), jnp.bfloat16),
        ),
        in_specs=[SMEM, SMEM] + [ANY] * len(arrays),
        out_specs=(VMEM, VMEM, VMEM, ANY, ANY),
        scratch_shapes=[
            pltpu.VMEM((kv_heads - near, early, HD), jnp.bfloat16),
            pltpu.VMEM((kv_heads - near, early, HD), jnp.bfloat16),
            pltpu.VMEM((2 * kv_heads, room, HD), jnp.float32),
            *[pltpu.VMEM(x.shape, jnp.bfloat16) for x in arrays[2:]],
            pltpu.SemaphoreType.DMA((len(arrays) - 2 + 2 * kv_heads + 4,)),
        ],
        compiler_params=grant(40 if branches > 16 else 20),
        cost_estimate=pl.CostEstimate(flops=0, bytes_accessed=8 * prompt_k.size, transcendentals=0),
        name="gather",
    )(me, prompt_mask, *arrays)
    halves, keys, values = lax.optimization_barrier((halves, keys, values))
    halves = halves + [across(x) for x in halves]
    cut = kv_heads * live + TILE
    halves = [part for x in halves for part in (x[:cut], x[cut:])]
    late = tail + split * result_rows + width
    outputs = pl.pallas_call(
        functools.partial(attend_kernel, split),
        out_shape=bf16(branches, CAP * heads, HD),
        in_specs=[SMEM] + [VMEM] * (4 + 2 * split) + [ANY] * 2,
        out_specs=VMEM,
        scratch_shapes=[
            pltpu.VMEM((kv_heads, late, HD), jnp.bfloat16),
            pltpu.VMEM((kv_heads, late, HD), jnp.bfloat16),
            pltpu.VMEM((chunk_rows, early - tail + late), jnp.float32),
            pltpu.VMEM((chunk_rows, early - tail + late), jnp.float32),
            pltpu.VMEM((kv_heads - near, early, HD), jnp.bfloat16),
            pltpu.VMEM((kv_heads - near, early, HD), jnp.bfloat16),
            pltpu.SemaphoreType.DMA((2,)),
        ],
        compiler_params=grant(40),
        cost_estimate=pl.CostEstimate(
            flops=4 * kv_heads * rows * HD * (early + width),
            bytes_accessed=4 * prompt_k.size,
            transcendentals=kv_heads * rows * (early + width),
        ),
        name="attend",
    )(me, keys, values, bias, recv, *halves, *[pltpu.with_memory_space_constraint(x, pltpu.HBM) for x in far_early])
    back = lax.all_to_all(outputs, "branch", split_axis=0, concat_axis=0, tiled=True)
    return pl.pallas_call(
        post_kernel,
        out_shape=jax.ShapeDtypeStruct((row_count, q_width), jnp.bfloat16),
        in_specs=[SMEM, VMEM],
        out_specs=VMEM,
        scratch_shapes=[
            pltpu.SMEM((branches,), jnp.int32),
            pltpu.VMEM((row_count, heads, HD), jnp.float32),
        ],
        compiler_params=grant(8),
        name="post",
    )(owner_of, back)


def solution(mesh):
    split = ("groups", "branch")
    in_specs = (
        P(split, None, None),
        P(split, None, None),
        P(split, None),
        P(split, None, None),
        P(split),
        P(split, None),
        P(split, None),
        P(split, None),
        P(split, None),
    )
    return jax.shard_map(body, mesh=mesh, in_specs=in_specs, out_specs=P(split, None), check_vma=False)
```

```python
import functools
import math

import jax
import jax.numpy as jnp
from jax import lax
from jax.experimental import pallas as pl
from jax.experimental.pallas import tpu as pltpu
from jax.sharding import PartitionSpec as P

HD = 128
GRP = 8
CAP = 2
TILE = 16
NONE = -1e30
ABSENT = 512.0
VMEM = pl.BlockSpec(memory_space=pltpu.VMEM)
SMEM = pl.BlockSpec(memory_space=pltpu.SMEM)
ANY = pl.BlockSpec(memory_space=pl.ANY)


def grant(mebibytes):
    return pltpu.CompilerParams(vmem_limit_bytes=mebibytes << 20)


def payload_kernel(pick_hbm, len_hbm, shared_hbm, out_ref, pick_ref, len_ref, shared_ref, sems):
    results, rows, width = shared_ref.shape
    branches = pick_ref.shape[1]
    moves = [
        pltpu.make_async_copy(source, target, sems.at[n])
        for n, (source, target) in enumerate(
            ((shared_hbm, shared_ref), (pick_hbm, pick_ref), (len_hbm, len_ref))
        )
    ]
    for move in moves:
        move.start()
    for move in moves:
        move.wait()
    live = results * rows
    lane = lax.broadcasted_iota(jnp.int32, (TILE, HD), 1)
    meta = jnp.zeros((TILE, HD), jnp.int32)
    for b in range(branches):
        meta = jnp.where(lane == b, pick_ref[0, b], meta)
    for r in range(results):
        meta = jnp.where(lane == branches + r, len_ref[0, r], meta)
    slabs = width // HD
    middle = slabs // 2 * live
    out_ref[middle : middle + TILE, :] = meta.astype(jnp.float32).astype(jnp.bfloat16)
    for j in range(slabs):
        part = shared_ref[:, :, j * HD : (j + 1) * HD].astype(jnp.float32)
        at = j * live + (TILE if 2 * j >= slabs else 0)
        out_ref[at : at + live, :] = part.reshape(live, HD).astype(jnp.bfloat16)


def place_rows(owner_ref, index_ref, count_ref):
    branches = count_ref.shape[0]
    for b in range(branches):
        count_ref[b] = 0
    for i in range(owner_ref.shape[0]):
        b = owner_ref[i]
        rank = count_ref[b]
        if index_ref is not None:
            index_ref[b * CAP + rank] = i
        count_ref[b] = rank + 1


def ring_place(me, chips):
    chip = me // 2
    return jnp.where(lax.rem(chip, 2) == 0, chip // 2, chips - 1 - chip // 2)


def has_short_way(me, chips):
    if chips != 8:
        return jnp.bool_(False)
    place = lax.rem(ring_place(me, chips), 4)
    return (place == 1) | (place == 2)


def prep_kernel(owner_ref, q_hbm, kv_hbm, after_hbm, out_ref, index_ref, count_ref, q_ref, kv_ref, q3_ref, kv3_ref, sems):
    del after_hbm
    rows, q_width = q_ref.shape
    branches = out_ref.shape[0]
    heads = q_width // HD
    kv_heads = heads // GRP
    moves = [
        pltpu.make_async_copy(q_hbm, q_ref, sems.at[0]),
        pltpu.make_async_copy(kv_hbm, kv_ref, sems.at[1]),
    ]
    for move in moves:
        move.start()
    for b in range(branches * CAP):
        index_ref[b] = 0
    place_rows(owner_ref, index_ref, count_ref)
    for move in moves:
        move.wait()
    q3_ref[...] = q_ref[...].astype(jnp.float32).reshape(rows, heads, HD)
    kv3_ref[...] = kv_ref[...].astype(jnp.float32).reshape(rows, 2 * kv_heads, HD)

    @pl.loop(0, branches)
    def _(b):
        index = [index_ref[b * CAP + c] for c in range(CAP)]
        parts = [q3_ref[i].reshape(kv_heads, 1, GRP, HD) for i in index]
        tiles = jnp.concatenate(parts, axis=1).reshape(heads * CAP, HD)
        pairs = [kv3_ref[i] for i in index]
        there = [count_ref[b] > c for c in range(CAP)]
        keys = [jnp.where(t, p[:kv_heads], ABSENT) for t, p in zip(there, pairs)]
        values = [jnp.where(t, p[kv_heads:], 0.0) for t, p in zip(there, pairs)]
        out_ref[b] = jnp.concatenate([tiles] + keys + values, axis=0).astype(jnp.bfloat16)


def dot_nt(a, b):
    return lax.dot_general(a, b, (((1,), (1,)), ((), ())), preferred_element_type=jnp.float32)


FACTOR = math.log2(math.e) / math.sqrt(HD)


def starter(sems):
    free = iter(range(sems.shape[0]))

    def start(source, target):
        copy = pltpu.make_async_copy(source, target, sems.at[next(free)])
        copy.start()
        return copy

    return start


def picked(meta, me, branches):
    lane = lax.broadcasted_iota(jnp.int32, (1, HD), 1)
    meta = meta.astype(jnp.float32)[0:1, :]
    pick = jnp.sum(jnp.where(lane == me, meta, 0.0)).astype(jnp.int32)
    length = jnp.sum(jnp.where(lane == branches + pick, meta, 0.0)).astype(jnp.int32)
    return pick, jnp.where(pick < 0, 0, length)


def rows_picked(slab, pick):
    both = slab.astype(jnp.float32)
    rows = slab.shape[0] // 2
    return jnp.where(pick == 0, both[0:rows], both[rows:])


def gather_kernel(whole, branches, short, me_ref, mask_ref, pk_hbm, pv_hbm, *refs):
    sources = refs[:whole]
    near_key, near_value, bias_ref, far_key_hbm, far_value_hbm = refs[whole : whole + 5]
    far_key, far_value, taken_ref, *blocks, sems = refs[whole + 5 :]
    near = near_key.shape[0]
    slabs, room, _ = taken_ref.shape
    kv_heads = slabs // 2
    prompt = pk_hbm.shape[1]
    live = (blocks[0].shape[0] - TILE) // slabs
    rows = live // 2
    middle = kv_heads * live
    start = starter(sems)
    moves = [start(source, target) for source, target in zip(sources, blocks)]
    wide = []
    homes = [(near_key.at[g], near_value.at[g]) for g in range(near)]
    homes += [(far_key.at[g], far_value.at[g]) for g in range(kv_heads - near)]
    for g, (key_ref, value_ref) in enumerate(homes):
        lanes = pl.ds(g * HD, HD)
        wide.append(start(pv_hbm.at[0, :, lanes], value_ref.at[pl.ds(0, prompt), :]))
        wide.append(start(pk_hbm.at[0, :, lanes], key_ref.at[pl.ds(0, prompt), :]))
    column = lax.broadcasted_iota(jnp.int32, (1, room), 1)
    seen = jnp.zeros((1, room), jnp.bool_)
    taken_ref[:, room - 2 * rows : room, :] = jnp.zeros((slabs, 2 * rows, HD), jnp.float32)
    for copy in moves:
        copy.wait()
    slot = jnp.int32(0)
    straight = has_short_way(me_ref[0], branches // 2)
    early = pl.ds(0, prompt)
    late = pl.ds(prompt, room)
    leaving = []
    for n, block in enumerate(blocks):
        if n == len(blocks) // 2:
            for copy in wide:
                copy.wait()
            leaving += [
                start(far_key.at[:, early, :], far_key_hbm.at[:, early, :]),
                start(far_value.at[:, early, :], far_value_hbm.at[:, early, :]),
            ]
        pick, length = picked(block[middle : middle + TILE, :], me_ref[0], branches)
        if n >= whole - short:
            pick, length = jnp.where(straight, pick, -1), jnp.where(straight, length, 0)
        at = pl.multiple_of(jnp.minimum(slot * rows, room - rows), 8)
        place = column - at
        seen = seen | ((place >= 0) & (place < length))

        @pl.when(pick >= 0)
        def _(block=block, pick=pick, at=at):
            for j in range(slabs):
                base = j * live + (TILE if j >= kv_heads else 0)
                taken_ref[j, pl.ds(at, rows), :] = rows_picked(block[base : base + live, :], pick)

        slot = slot + (pick >= 0).astype(jnp.int32)
    for g, (key_ref, value_ref) in enumerate(homes):
        key_ref[prompt : prompt + room, :] = taken_ref[g].astype(jnp.bfloat16)
        value_ref[prompt : prompt + room, :] = taken_ref[kv_heads + g].astype(jnp.bfloat16)
    leaving += [
        start(far_key.at[:, late, :], far_key_hbm.at[:, late, :]),
        start(far_value.at[:, late, :], far_value_hbm.at[:, late, :]),
    ]
    blocks_seen = mask_ref.shape[1]
    biases = [
        jnp.full((1, prompt // blocks_seen), jnp.where(mask_ref[0, j] > 0, 0.0, NONE))
        for j in range(blocks_seen)
    ]
    bias = jnp.concatenate(biases + [jnp.where(seen, 0.0, NONE)], axis=1)
    bias_ref[...] = bias
    for copy in leaving:
        copy.wait()


def attend_kernel(split, me_ref, near_key, near_value, bias_ref, recv_ref, *refs):
    halves = refs[: 2 * split]
    far_key_hbm, far_value_hbm, out_ref, late_key_ref, late_value_ref, first_ref, second_ref, far_key, far_value, sems = (
        refs[2 * split :]
    )
    near, early, _ = near_key.shape
    kv_heads = near + far_key.shape[0]
    early_of = [(near_key.at[g], near_value.at[g]) for g in range(near)]
    early_of += [(far_key.at[g], far_value.at[g]) for g in range(kv_heads - near)]
    start = starter(sems)
    far_moves = [start(far_key_hbm, far_key), start(far_value_hbm, far_value)]
    branches = recv_ref.shape[0]
    heads = kv_heads * GRP
    width = branches * CAP
    late = late_key_ref.shape[1]
    live = halves[1].shape[0] // kv_heads
    far = live // 2
    tail = late - width - split * far
    main = early - tail
    chunk = min(branches, 16)
    count = chunk * TILE

    def score(g, base, target):
        queries = recv_ref[pl.ds(base, chunk), g * TILE : (g + 1) * TILE, :].reshape(count, HD)
        target[:, 0:main] = dot_nt(queries, early_of[g][0][0:main, :]) + bias_ref[0:1, 0:main]

    if branches == chunk:
        score(0, 0, first_ref)
        score(1, 0, second_ref)
    size = branches * TILE
    place = lax.broadcasted_iota(jnp.int32, (size, size), 1)
    wanted = lax.broadcasted_iota(jnp.int32, (size, size), 0)
    choose = jnp.where(place == lax.rem(wanted, width) * kv_heads + wanted // width, 1.0, 0.0).astype(jnp.bfloat16)
    unique = []
    for which in range(2):
        first = heads * CAP + which * TILE
        rows = recv_ref[:, first : first + TILE, :].reshape(size, HD)
        unique.append(jnp.dot(choose, rows, preferred_element_type=jnp.float32).reshape(kv_heads, width, HD))
    choices = [picked(halves[2 * n][kv_heads * live :, :], me_ref[0], branches) for n in range(split)]
    straight = has_short_way(me_ref[0], branches // 2)
    choices = [(pick, jnp.where(straight, 0, length)) for pick, length in choices]

    def fill(g):
        for which, target in ((0, late_key_ref), (1, late_value_ref)):
            rows = [rows_picked(halves[2 * n + which][g * live : (g + 1) * live, :], choices[n][0]) for n in range(split)]
            if tail:
                rows = [early_of[g][which][main:early, :].astype(jnp.float32)] + rows
            target[g] = jnp.concatenate(rows + [unique[which][g]], axis=0).astype(jnp.bfloat16)

    for g in range(near):
        fill(g)
    one = jnp.where(lax.broadcasted_iota(jnp.int32, (TILE, HD), 1) == 0, 1.0, 0.0).astype(jnp.bfloat16)
    absent = dot_nt(one, late_key_ref[0])[0:1, :] > ABSENT / 2
    spot = lax.broadcasted_iota(jnp.int32, (1, far), 1)
    late_bias = [jnp.where(spot < length, 0.0, NONE) for _, length in choices]
    if tail:
        late_bias = [bias_ref[0:1, main:early]] + late_bias
    late_bias = jnp.concatenate(late_bias + [jnp.zeros((1, width), jnp.float32)], axis=1)
    column = lax.broadcasted_iota(jnp.int32, (count, late), 1) - (late - width)
    own_slot = lax.broadcasted_iota(jnp.int32, (count, late), 0) // GRP

    def far_part():
        for copy in far_moves:
            copy.wait()
        for g in range(near, kv_heads):
            fill(g)

    if branches > chunk:
        far_part()

    def run(base):
        late_hidden = jnp.where((column >= 0) & (absent | (column > own_slot + base * CAP)), NONE, late_bias)

        def score_late(g, target):
            queries = recv_ref[pl.ds(base, chunk), g * TILE : (g + 1) * TILE, :].reshape(count, HD)
            target[:, main : main + late] = dot_nt(queries, late_key_ref[g]) + late_hidden

        def finish(g, source):
            scores = source[...]
            largest = jnp.max(scores, axis=1, keepdims=True)
            weights = jnp.exp2((scores - largest) * FACTOR)
            total = jnp.sum(weights, axis=1, keepdims=True)
            probs = weights.astype(jnp.bfloat16)
            mixed = jnp.dot(probs[:, 0:main], early_of[g][1][0:main, :], preferred_element_type=jnp.float32)
            mixed = mixed + jnp.dot(probs[:, main:], late_value_ref[g], preferred_element_type=jnp.float32)
            result = (mixed / total).astype(jnp.bfloat16)
            out_ref[pl.ds(base, chunk), g * TILE : (g + 1) * TILE, :] = result.reshape(chunk, TILE, HD)

        buffers = (first_ref, second_ref)
        if branches > chunk:
            score(0, base, buffers[0])
            score(1, base, buffers[1])
        score_late(0, buffers[0])
        score_late(1, buffers[1])
        for g in range(kv_heads):
            finish(g, buffers[g % 2])
            if g + 2 == near and branches == chunk:
                far_part()
            if g + 2 < kv_heads:
                score(g + 2, base, buffers[g % 2])
                score_late(g + 2, buffers[g % 2])

    if branches == chunk:
        run(0)
    else:
        @pl.loop(0, branches // chunk)
        def _(part):
            run(part * chunk)


def post_kernel(owner_ref, back_ref, out_ref, count_ref, o3_ref):
    rows, width = out_ref.shape
    heads = width // HD
    branches = back_ref.shape[0]
    for b in range(branches):
        count_ref[b] = 0

    @pl.loop(0, rows)
    def _(i):
        b = owner_ref[i]
        rank = count_ref[b]
        count_ref[b] = rank + 1
        tiles = back_ref[b].astype(jnp.float32).reshape(heads // GRP, CAP, GRP, HD)
        o3_ref[i] = jnp.where(rank == 0, tiles[:, 0], tiles[:, 1]).reshape(heads, HD)

    out_ref[...] = o3_ref[...].reshape(rows, width).astype(jnp.bfloat16)


def body(
    prompt_k, prompt_v, prompt_mask, shared_kv, shared_len, send_pick, unique_q, unique_kv, unique_owner
):
    branches = lax.axis_size("branch")
    chips = branches // 2
    row_count, q_width = unique_q.shape
    heads = q_width // HD
    kv_width = unique_kv.shape[1] // 2
    kv_heads = kv_width // HD
    results, result_rows, _ = shared_kv.shape
    owner_of = unique_owner[:, 0]
    live = results * result_rows
    slot_rows = CAP * heads + 2 * TILE

    def bf16(*shape):
        return jax.ShapeDtypeStruct(shape, jnp.bfloat16)

    block = pl.pallas_call(
        payload_kernel,
        out_shape=bf16(2 * kv_heads * live + TILE, HD),
        in_specs=[ANY] * 3,
        out_specs=VMEM,
        scratch_shapes=[
            pltpu.SMEM(send_pick.shape, jnp.int32),
            pltpu.SMEM((1, results), jnp.int32),
            pltpu.VMEM(shared_kv.shape, jnp.bfloat16),
            pltpu.SemaphoreType.DMA((3,)),
        ],
        compiler_params=grant(56),
        name="payload",
    )(send_pick, shared_len.reshape(1, results), shared_kv)

    order = list(range(0, chips, 2)) + list(range(1, chips, 2))[::-1]

    def hop(x, places):
        pairs = [(order[p] * 2 + core, order[q] * 2 + core) for p, q in places for core in range(2)]
        return lax.ppermute(x, "branch", pairs)

    def along(x, step):
        return hop(x, [(p, (p + step) % chips) for p in range(chips)])

    def across(x):
        return lax.ppermute(x, "branch", [(i, i ^ 1) for i in range(branches)])

    send = pl.pallas_call(
        prep_kernel,
        out_shape=bf16(branches, slot_rows, HD),
        in_specs=[SMEM, ANY, ANY, ANY],
        out_specs=VMEM,
        scratch_shapes=[
            pltpu.SMEM((branches * CAP,), jnp.int32),
            pltpu.SMEM((branches,), jnp.int32),
            pltpu.VMEM(unique_q.shape, jnp.bfloat16),
            pltpu.VMEM(unique_kv.shape, jnp.bfloat16),
            pltpu.VMEM((row_count, heads, HD), jnp.float32),
            pltpu.VMEM((row_count, 2 * kv_heads, HD), jnp.float32),
            pltpu.SemaphoreType.DMA((2,)),
        ],
        compiler_params=grant(56),
        cost_estimate=pl.CostEstimate(flops=0, bytes_accessed=1024, transcendentals=0),
        name="prep",
    )(owner_of, unique_q, unique_kv, block)

    me = jnp.full((1,), lax.axis_index("branch"), jnp.int32)
    blocks, shorts = [block], []
    ahead = behind = block
    for step in range(chips // 2 - 1):
        ahead, behind = along(ahead, 1), along(behind, -1)
        blocks += [ahead, behind]
        if step == 0:
            send, ahead = lax.optimization_barrier((send, ahead))
        if step == 0 and chips == 8:
            place = lax.rem(ring_place(me[0], chips), 4)
            facing = jnp.where(place == 2, ahead, behind)
            shorts = [hop(facing, [(1, 6), (6, 1), (2, 5), (5, 2)])]
    send, ahead, behind, *shorts = lax.optimization_barrier((send, ahead, behind, *shorts))
    recv = lax.all_to_all(send, "branch", split_axis=0, concat_axis=0, tiled=True)
    if shorts:
        last = jnp.where(lax.rem(ring_place(me[0], chips), 4) == 0, behind, ahead)
        halves = [hop(last, [(7, 0), (0, 7), (3, 4), (4, 3)])]
    else:
        halves = [along(ahead, 1)]
    shorts = shorts + [across(x) for x in shorts]
    blocks = blocks + [across(x) for x in blocks] + shorts
    prompt = prompt_k.shape[1]
    whole, split = len(blocks), 2
    room = branches * 3 // 4 * result_rows
    early = prompt + room
    width = CAP * branches
    tail = early % HD
    chunk_rows = min(branches, 16) * TILE
    rows = width * GRP
    arrays = [pltpu.with_memory_space_constraint(x, pltpu.HBM) for x in (prompt_k, prompt_v, *blocks)]
    near = kv_heads // 2 - 1
    keys, values, bias, *far_early = pl.pallas_call(
        functools.partial(gather_kernel, whole, branches, len(shorts)),
        out_shape=(
            pltpu.VMEM((near, early, HD), jnp.bfloat16),
            pltpu.VMEM((near, early, HD), jnp.bfloat16),
            pltpu.VMEM((1, early), jnp.float32),
            pltpu.HBM((kv_heads - near, early, HD), jnp.bfloat16),
            pltpu.HBM((kv_heads - near, early, HD), jnp.bfloat16),
        ),
        in_specs=[SMEM, SMEM] + [ANY] * len(arrays),
        out_specs=(VMEM, VMEM, VMEM, ANY, ANY),
        scratch_shapes=[
            pltpu.VMEM((kv_heads - near, early, HD), jnp.bfloat16),
            pltpu.VMEM((kv_heads - near, early, HD), jnp.bfloat16),
            pltpu.VMEM((2 * kv_heads, room, HD), jnp.float32),
            *[pltpu.VMEM(x.shape, jnp.bfloat16) for x in arrays[2:]],
            pltpu.SemaphoreType.DMA((len(arrays) - 2 + 2 * kv_heads + 4,)),
        ],
        compiler_params=grant(40 if branches > 16 else 20),
        cost_estimate=pl.CostEstimate(flops=0, bytes_accessed=8 * prompt_k.size, transcendentals=0),
        name="gather",
    )(me, prompt_mask, *arrays)
    halves, keys, values = lax.optimization_barrier((halves, keys, values))
    halves = halves + [across(x) for x in halves]
    cut = kv_heads * live + TILE
    halves = [part for x in halves for part in (x[:cut], x[cut:])]
    late = tail + split * result_rows + width
    outputs = pl.pallas_call(
        functools.partial(attend_kernel, split),
        out_shape=bf16(branches, CAP * heads, HD),
        in_specs=[SMEM] + [VMEM] * (4 + 2 * split) + [ANY] * 2,
        out_specs=VMEM,
        scratch_shapes=[
            pltpu.VMEM((kv_heads, late, HD), jnp.bfloat16),
            pltpu.VMEM((kv_heads, late, HD), jnp.bfloat16),
            pltpu.VMEM((chunk_rows, early - tail + late), jnp.float32),
            pltpu.VMEM((chunk_rows, early - tail + late), jnp.float32),
            pltpu.VMEM((kv_heads - near, early, HD), jnp.bfloat16),
            pltpu.VMEM((kv_heads - near, early, HD), jnp.bfloat16),
            pltpu.SemaphoreType.DMA((2,)),
        ],
        compiler_params=grant(40),
        cost_estimate=pl.CostEstimate(
            flops=4 * kv_heads * rows * HD * (early + width),
            bytes_accessed=4 * prompt_k.size,
            transcendentals=kv_heads * rows * (early + width),
        ),
        name="attend",
    )(me, keys, values, bias, recv, *halves, *[pltpu.with_memory_space_constraint(x, pltpu.HBM) for x in far_early])
    back = lax.all_to_all(outputs, "branch", split_axis=0, concat_axis=0, tiled=True)
    return pl.pallas_call(
        post_kernel,
        out_shape=jax.ShapeDtypeStruct((row_count, q_width), jnp.bfloat16),
        in_specs=[SMEM, VMEM],
        out_specs=VMEM,
        scratch_shapes=[
            pltpu.SMEM((branches,), jnp.int32),
            pltpu.VMEM((row_count, heads, HD), jnp.float32),
        ],
        compiler_params=grant(8),
        name="post",
    )(owner_of, back)


def solution(mesh):
    split = ("groups", "branch")
    in_specs = (
        P(split, None, None),
        P(split, None, None),
        P(split, None),
        P(split, None, None),
        P(split),
        P(split, None),
        P(split, None),
        P(split, None),
        P(split, None),
    )
    return jax.shard_map(body, mesh=mesh, in_specs=in_specs, out_specs=P(split, None), check_vma=False)
```

```python
import functools
import math

import jax
import jax.numpy as jnp
from jax import lax
from jax.experimental import pallas as pl
from jax.experimental.pallas import tpu as pltpu
from jax.sharding import PartitionSpec as P

HD = 128
GRP = 8
CAP = 2
TILE = 16
NONE = -1e30
ABSENT = 512.0
VMEM = pl.BlockSpec(memory_space=pltpu.VMEM)
SMEM = pl.BlockSpec(memory_space=pltpu.SMEM)
ANY = pl.BlockSpec(memory_space=pl.ANY)


def grant(mebibytes):
    return pltpu.CompilerParams(vmem_limit_bytes=mebibytes << 20)


def payload_kernel(pick_hbm, len_hbm, shared_hbm, out_ref, pick_ref, len_ref, shared_ref, sems):
    results, rows, width = shared_ref.shape
    branches = pick_ref.shape[1]
    moves = [
        pltpu.make_async_copy(source, target, sems.at[n])
        for n, (source, target) in enumerate(
            ((shared_hbm, shared_ref), (pick_hbm, pick_ref), (len_hbm, len_ref))
        )
    ]
    for move in moves:
        move.start()
    for move in moves:
        move.wait()
    live = results * rows
    lane = lax.broadcasted_iota(jnp.int32, (TILE, HD), 1)
    meta = jnp.zeros((TILE, HD), jnp.int32)
    for b in range(branches):
        meta = jnp.where(lane == b, pick_ref[0, b], meta)
    for r in range(results):
        meta = jnp.where(lane == branches + r, len_ref[0, r], meta)
    slabs = width // HD
    middle = slabs // 2 * live
    out_ref[middle : middle + TILE, :] = meta.astype(jnp.float32).astype(jnp.bfloat16)
    for j in range(slabs):
        part = shared_ref[:, :, j * HD : (j + 1) * HD].astype(jnp.float32)
        at = j * live + (TILE if 2 * j >= slabs else 0)
        out_ref[at : at + live, :] = part.reshape(live, HD).astype(jnp.bfloat16)


def place_rows(owner_ref, index_ref, count_ref):
    branches = count_ref.shape[0]
    for b in range(branches):
        count_ref[b] = 0
    for i in range(owner_ref.shape[0]):
        b = owner_ref[i]
        rank = count_ref[b]
        if index_ref is not None:
            index_ref[b * CAP + rank] = i
        count_ref[b] = rank + 1


def ring_place(me, chips):
    chip = me // 2
    return jnp.where(lax.rem(chip, 2) == 0, chip // 2, chips - 1 - chip // 2)


def has_short_way(me, chips):
    if chips != 8:
        return jnp.bool_(False)
    place = lax.rem(ring_place(me, chips), 4)
    return (place == 1) | (place == 2)


def prep_kernel(owner_ref, q_hbm, kv_hbm, after_hbm, out_ref, index_ref, count_ref, q_ref, kv_ref, q3_ref, kv3_ref, sems):
    del after_hbm
    rows, q_width = q_ref.shape
    branches = out_ref.shape[0]
    heads = q_width // HD
    kv_heads = heads // GRP
    moves = [
        pltpu.make_async_copy(q_hbm, q_ref, sems.at[0]),
        pltpu.make_async_copy(kv_hbm, kv_ref, sems.at[1]),
    ]
    for move in moves:
        move.start()
    for b in range(branches * CAP):
        index_ref[b] = 0
    place_rows(owner_ref, index_ref, count_ref)
    for move in moves:
        move.wait()
    q3_ref[...] = q_ref[...].astype(jnp.float32).reshape(rows, heads, HD)
    kv3_ref[...] = kv_ref[...].astype(jnp.float32).reshape(rows, 2 * kv_heads, HD)

    @pl.loop(0, branches)
    def _(b):
        index = [index_ref[b * CAP + c] for c in range(CAP)]
        parts = [q3_ref[i].reshape(kv_heads, 1, GRP, HD) for i in index]
        tiles = jnp.concatenate(parts, axis=1).reshape(heads * CAP, HD)
        pairs = [kv3_ref[i] for i in index]
        there = [count_ref[b] > c for c in range(CAP)]
        keys = [jnp.where(t, p[:kv_heads], ABSENT) for t, p in zip(there, pairs)]
        values = [jnp.where(t, p[kv_heads:], 0.0) for t, p in zip(there, pairs)]
        out_ref[b] = jnp.concatenate([tiles] + keys + values, axis=0).astype(jnp.bfloat16)


def dot_nt(a, b):
    return lax.dot_general(a, b, (((1,), (1,)), ((), ())), preferred_element_type=jnp.float32)


FACTOR = math.log2(math.e) / math.sqrt(HD)


def starter(sems):
    free = iter(range(sems.shape[0]))

    def start(source, target):
        copy = pltpu.make_async_copy(source, target, sems.at[next(free)])
        copy.start()
        return copy

    return start


def picked(meta, me, branches):
    lane = lax.broadcasted_iota(jnp.int32, (1, HD), 1)
    meta = meta.astype(jnp.float32)[0:1, :]
    pick = jnp.sum(jnp.where(lane == me, meta, 0.0)).astype(jnp.int32)
    length = jnp.sum(jnp.where(lane == branches + pick, meta, 0.0)).astype(jnp.int32)
    return pick, jnp.where(pick < 0, 0, length)


def rows_picked(slab, pick):
    both = slab.astype(jnp.float32)
    rows = slab.shape[0] // 2
    return jnp.where(pick == 0, both[0:rows], both[rows:])


def gather_kernel(whole, branches, short, me_ref, mask_ref, pk_hbm, pv_hbm, *refs):
    sources = refs[:whole]
    near_key, near_value, bias_ref, far_key_hbm, far_value_hbm = refs[whole : whole + 5]
    far_key, far_value, taken_ref, *blocks, sems = refs[whole + 5 :]
    near = near_key.shape[0]
    slabs, room, _ = taken_ref.shape
    kv_heads = slabs // 2
    prompt = pk_hbm.shape[1]
    live = (blocks[0].shape[0] - TILE) // slabs
    rows = live // 2
    middle = kv_heads * live
    start = starter(sems)
    moves = [start(source, target) for source, target in zip(sources, blocks)]
    wide = []
    homes = [(near_key.at[g], near_value.at[g]) for g in range(near)]
    homes += [(far_key.at[g], far_value.at[g]) for g in range(kv_heads - near)]
    for g, (key_ref, value_ref) in enumerate(homes):
        lanes = pl.ds(g * HD, HD)
        wide.append(start(pv_hbm.at[0, :, lanes], value_ref.at[pl.ds(0, prompt), :]))
        wide.append(start(pk_hbm.at[0, :, lanes], key_ref.at[pl.ds(0, prompt), :]))
    column = lax.broadcasted_iota(jnp.int32, (1, room), 1)
    seen = jnp.zeros((1, room), jnp.bool_)
    taken_ref[:, room - 2 * rows : room, :] = jnp.zeros((slabs, 2 * rows, HD), jnp.float32)
    for copy in moves:
        copy.wait()
    slot = jnp.int32(0)
    straight = has_short_way(me_ref[0], branches // 2)
    early = pl.ds(0, prompt)
    late = pl.ds(prompt, room)
    leaving = []
    for n, block in enumerate(blocks):
        if n == len(blocks) * 3 // 4:
            for copy in wide:
                copy.wait()
            leaving += [
                start(far_key.at[:, early, :], far_key_hbm.at[:, early, :]),
                start(far_value.at[:, early, :], far_value_hbm.at[:, early, :]),
            ]
        pick, length = picked(block[middle : middle + TILE, :], me_ref[0], branches)
        if n >= whole - short:
            pick, length = jnp.where(straight, pick, -1), jnp.where(straight, length, 0)
        at = pl.multiple_of(jnp.minimum(slot * rows, room - rows), 8)
        place = column - at
        seen = seen | ((place >= 0) & (place < length))

        @pl.when(pick >= 0)
        def _(block=block, pick=pick, at=at):
            for j in range(slabs):
                base = j * live + (TILE if j >= kv_heads else 0)
                taken_ref[j, pl.ds(at, rows), :] = rows_picked(block[base : base + live, :], pick)

        slot = slot + (pick >= 0).astype(jnp.int32)
    for g, (key_ref, value_ref) in enumerate(homes):
        key_ref[prompt : prompt + room, :] = taken_ref[g].astype(jnp.bfloat16)
        value_ref[prompt : prompt + room, :] = taken_ref[kv_heads + g].astype(jnp.bfloat16)
    leaving += [
        start(far_key.at[:, late, :], far_key_hbm.at[:, late, :]),
        start(far_value.at[:, late, :], far_value_hbm.at[:, late, :]),
    ]
    blocks_seen = mask_ref.shape[1]
    biases = [
        jnp.full((1, prompt // blocks_seen), jnp.where(mask_ref[0, j] > 0, 0.0, NONE))
        for j in range(blocks_seen)
    ]
    bias = jnp.concatenate(biases + [jnp.where(seen, 0.0, NONE)], axis=1)
    bias_ref[...] = bias
    for copy in leaving:
        copy.wait()


def attend_kernel(split, me_ref, near_key, near_value, bias_ref, recv_ref, *refs):
    halves = refs[: 2 * split]
    far_key_hbm, far_value_hbm, out_ref, late_key_ref, late_value_ref, first_ref, second_ref, far_key, far_value, sems = (
        refs[2 * split :]
    )
    near, early, _ = near_key.shape
    kv_heads = near + far_key.shape[0]
    early_of = [(near_key.at[g], near_value.at[g]) for g in range(near)]
    early_of += [(far_key.at[g], far_value.at[g]) for g in range(kv_heads - near)]
    start = starter(sems)
    far_moves = [start(far_key_hbm, far_key), start(far_value_hbm, far_value)]
    branches = recv_ref.shape[0]
    heads = kv_heads * GRP
    width = branches * CAP
    late = late_key_ref.shape[1]
    live = halves[1].shape[0] // kv_heads
    far = live // 2
    tail = late - width - split * far
    main = early - tail
    chunk = min(branches, 16)
    count = chunk * TILE

    def score(g, base, target):
        queries = recv_ref[pl.ds(base, chunk), g * TILE : (g + 1) * TILE, :].reshape(count, HD)
        target[:, 0:main] = dot_nt(queries, early_of[g][0][0:main, :]) + bias_ref[0:1, 0:main]

    if branches == chunk:
        score(0, 0, first_ref)
        score(1, 0, second_ref)
    size = branches * TILE
    place = lax.broadcasted_iota(jnp.int32, (size, size), 1)
    wanted = lax.broadcasted_iota(jnp.int32, (size, size), 0)
    choose = jnp.where(place == lax.rem(wanted, width) * kv_heads + wanted // width, 1.0, 0.0).astype(jnp.bfloat16)
    unique = []
    for which in range(2):
        first = heads * CAP + which * TILE
        rows = recv_ref[:, first : first + TILE, :].reshape(size, HD)
        unique.append(jnp.dot(choose, rows, preferred_element_type=jnp.float32).reshape(kv_heads, width, HD))
    choices = [picked(halves[2 * n][kv_heads * live :, :], me_ref[0], branches) for n in range(split)]
    straight = has_short_way(me_ref[0], branches // 2)
    choices = [(pick, jnp.where(straight, 0, length)) for pick, length in choices]

    def fill(g):
        for which, target in ((0, late_key_ref), (1, late_value_ref)):
            rows = [rows_picked(halves[2 * n + which][g * live : (g + 1) * live, :], choices[n][0]) for n in range(split)]
            if tail:
                rows = [early_of[g][which][main:early, :].astype(jnp.float32)] + rows
            target[g] = jnp.concatenate(rows + [unique[which][g]], axis=0).astype(jnp.bfloat16)

    for g in range(near):
        fill(g)
    one = jnp.where(lax.broadcasted_iota(jnp.int32, (TILE, HD), 1) == 0, 1.0, 0.0).astype(jnp.bfloat16)
    absent = dot_nt(one, late_key_ref[0])[0:1, :] > ABSENT / 2
    spot = lax.broadcasted_iota(jnp.int32, (1, far), 1)
    late_bias = [jnp.where(spot < length, 0.0, NONE) for _, length in choices]
    if tail:
        late_bias = [bias_ref[0:1, main:early]] + late_bias
    late_bias = jnp.concatenate(late_bias + [jnp.zeros((1, width), jnp.float32)], axis=1)
    column = lax.broadcasted_iota(jnp.int32, (count, late), 1) - (late - width)
    own_slot = lax.broadcasted_iota(jnp.int32, (count, late), 0) // GRP

    def far_part():
        for copy in far_moves:
            copy.wait()
        for g in range(near, kv_heads):
            fill(g)

    if branches > chunk:
        far_part()

    def run(base):
        late_hidden = jnp.where((column >= 0) & (absent | (column > own_slot + base * CAP)), NONE, late_bias)

        def score_late(g, target):
            queries = recv_ref[pl.ds(base, chunk), g * TILE : (g + 1) * TILE, :].reshape(count, HD)
            target[:, main : main + late] = dot_nt(queries, late_key_ref[g]) + late_hidden

        def finish(g, source):
            scores = source[...]
            largest = jnp.max(scores, axis=1, keepdims=True)
            weights = jnp.exp2((scores - largest) * FACTOR)
            total = jnp.sum(weights, axis=1, keepdims=True)
            probs = weights.astype(jnp.bfloat16)
            mixed = jnp.dot(probs[:, 0:main], early_of[g][1][0:main, :], preferred_element_type=jnp.float32)
            mixed = mixed + jnp.dot(probs[:, main:], late_value_ref[g], preferred_element_type=jnp.float32)
            result = (mixed / total).astype(jnp.bfloat16)
            out_ref[pl.ds(base, chunk), g * TILE : (g + 1) * TILE, :] = result.reshape(chunk, TILE, HD)

        buffers = (first_ref, second_ref)
        if branches > chunk:
            score(0, base, buffers[0])
            score(1, base, buffers[1])
        score_late(0, buffers[0])
        score_late(1, buffers[1])
        for g in range(kv_heads):
            finish(g, buffers[g % 2])
            if g + 2 == near and branches == chunk:
                far_part()
            if g + 2 < kv_heads:
                score(g + 2, base, buffers[g % 2])
                score_late(g + 2, buffers[g % 2])

    if branches == chunk:
        run(0)
    else:
        @pl.loop(0, branches // chunk)
        def _(part):
            run(part * chunk)


def post_kernel(owner_ref, back_ref, out_ref, count_ref, o3_ref):
    rows, width = out_ref.shape
    heads = width // HD
    branches = back_ref.shape[0]
    for b in range(branches):
        count_ref[b] = 0

    @pl.loop(0, rows)
    def _(i):
        b = owner_ref[i]
        rank = count_ref[b]
        count_ref[b] = rank + 1
        tiles = back_ref[b].astype(jnp.float32).reshape(heads // GRP, CAP, GRP, HD)
        o3_ref[i] = jnp.where(rank == 0, tiles[:, 0], tiles[:, 1]).reshape(heads, HD)

    out_ref[...] = o3_ref[...].reshape(rows, width).astype(jnp.bfloat16)


def body(
    prompt_k, prompt_v, prompt_mask, shared_kv, shared_len, send_pick, unique_q, unique_kv, unique_owner
):
    branches = lax.axis_size("branch")
    chips = branches // 2
    row_count, q_width = unique_q.shape
    heads = q_width // HD
    kv_width = unique_kv.shape[1] // 2
    kv_heads = kv_width // HD
    results, result_rows, _ = shared_kv.shape
    owner_of = unique_owner[:, 0]
    live = results * result_rows
    slot_rows = CAP * heads + 2 * TILE

    def bf16(*shape):
        return jax.ShapeDtypeStruct(shape, jnp.bfloat16)

    block = pl.pallas_call(
        payload_kernel,
        out_shape=bf16(2 * kv_heads * live + TILE, HD),
        in_specs=[ANY] * 3,
        out_specs=VMEM,
        scratch_shapes=[
            pltpu.SMEM(send_pick.shape, jnp.int32),
            pltpu.SMEM((1, results), jnp.int32),
            pltpu.VMEM(shared_kv.shape, jnp.bfloat16),
            pltpu.SemaphoreType.DMA((3,)),
        ],
        compiler_params=grant(56),
        name="payload",
    )(send_pick, shared_len.reshape(1, results), shared_kv)

    order = list(range(0, chips, 2)) + list(range(1, chips, 2))[::-1]

    def hop(x, places):
        pairs = [(order[p] * 2 + core, order[q] * 2 + core) for p, q in places for core in range(2)]
        return lax.ppermute(x, "branch", pairs)

    def along(x, step):
        return hop(x, [(p, (p + step) % chips) for p in range(chips)])

    def across(x):
        return lax.ppermute(x, "branch", [(i, i ^ 1) for i in range(branches)])

    send = pl.pallas_call(
        prep_kernel,
        out_shape=bf16(branches, slot_rows, HD),
        in_specs=[SMEM, ANY, ANY, ANY],
        out_specs=VMEM,
        scratch_shapes=[
            pltpu.SMEM((branches * CAP,), jnp.int32),
            pltpu.SMEM((branches,), jnp.int32),
            pltpu.VMEM(unique_q.shape, jnp.bfloat16),
            pltpu.VMEM(unique_kv.shape, jnp.bfloat16),
            pltpu.VMEM((row_count, heads, HD), jnp.float32),
            pltpu.VMEM((row_count, 2 * kv_heads, HD), jnp.float32),
            pltpu.SemaphoreType.DMA((2,)),
        ],
        compiler_params=grant(56),
        cost_estimate=pl.CostEstimate(flops=0, bytes_accessed=1024, transcendentals=0),
        name="prep",
    )(owner_of, unique_q, unique_kv, block)

    me = jnp.full((1,), lax.axis_index("branch"), jnp.int32)
    blocks, shorts = [block], []
    ahead = behind = block
    for step in range(chips // 2 - 1):
        ahead, behind = along(ahead, 1), along(behind, -1)
        blocks += [ahead, behind]
        if step == 0:
            send, ahead = lax.optimization_barrier((send, ahead))
        if step == 0 and chips == 8:
            place = lax.rem(ring_place(me[0], chips), 4)
            facing = jnp.where(place == 2, ahead, behind)
            shorts = [hop(facing, [(1, 6), (6, 1), (2, 5), (5, 2)])]
    send, ahead, behind, *shorts = lax.optimization_barrier((send, ahead, behind, *shorts))
    recv = lax.all_to_all(send, "branch", split_axis=0, concat_axis=0, tiled=True)
    if shorts:
        last = jnp.where(lax.rem(ring_place(me[0], chips), 4) == 0, behind, ahead)
        halves = [hop(last, [(7, 0), (0, 7), (3, 4), (4, 3)])]
    else:
        halves = [along(ahead, 1)]
    shorts = shorts + [across(x) for x in shorts]
    blocks = blocks + [across(x) for x in blocks] + shorts
    prompt = prompt_k.shape[1]
    whole, split = len(blocks), 2
    room = branches * 3 // 4 * result_rows
    early = prompt + room
    width = CAP * branches
    tail = early % HD
    chunk_rows = min(branches, 16) * TILE
    rows = width * GRP
    arrays = [pltpu.with_memory_space_constraint(x, pltpu.HBM) for x in (prompt_k, prompt_v, *blocks)]
    near = kv_heads // 2 - 1
    keys, values, bias, *far_early = pl.pallas_call(
        functools.partial(gather_kernel, whole, branches, len(shorts)),
        out_shape=(
            pltpu.VMEM((near, early, HD), jnp.bfloat16),
            pltpu.VMEM((near, early, HD), jnp.bfloat16),
            pltpu.VMEM((1, early), jnp.float32),
            pltpu.HBM((kv_heads - near, early, HD), jnp.bfloat16),
            pltpu.HBM((kv_heads - near, early, HD), jnp.bfloat16),
        ),
        in_specs=[SMEM, SMEM] + [ANY] * len(arrays),
        out_specs=(VMEM, VMEM, VMEM, ANY, ANY),
        scratch_shapes=[
            pltpu.VMEM((kv_heads - near, early, HD), jnp.bfloat16),
            pltpu.VMEM((kv_heads - near, early, HD), jnp.bfloat16),
            pltpu.VMEM((2 * kv_heads, room, HD), jnp.float32),
            *[pltpu.VMEM(x.shape, jnp.bfloat16) for x in arrays[2:]],
            pltpu.SemaphoreType.DMA((len(arrays) - 2 + 2 * kv_heads + 4,)),
        ],
        compiler_params=grant(40 if branches > 16 else 20),
        cost_estimate=pl.CostEstimate(flops=0, bytes_accessed=8 * prompt_k.size, transcendentals=0),
        name="gather",
    )(me, prompt_mask, *arrays)
    halves, keys, values = lax.optimization_barrier((halves, keys, values))
    halves = halves + [across(x) for x in halves]
    cut = kv_heads * live + TILE
    halves = [part for x in halves for part in (x[:cut], x[cut:])]
    late = tail + split * result_rows + width
    outputs = pl.pallas_call(
        functools.partial(attend_kernel, split),
        out_shape=bf16(branches, CAP * heads, HD),
        in_specs=[SMEM] + [VMEM] * (4 + 2 * split) + [ANY] * 2,
        out_specs=VMEM,
        scratch_shapes=[
            pltpu.VMEM((kv_heads, late, HD), jnp.bfloat16),
            pltpu.VMEM((kv_heads, late, HD), jnp.bfloat16),
            pltpu.VMEM((chunk_rows, early - tail + late), jnp.float32),
            pltpu.VMEM((chunk_rows, early - tail + late), jnp.float32),
            pltpu.VMEM((kv_heads - near, early, HD), jnp.bfloat16),
            pltpu.VMEM((kv_heads - near, early, HD), jnp.bfloat16),
            pltpu.SemaphoreType.DMA((2,)),
        ],
        compiler_params=grant(40),
        cost_estimate=pl.CostEstimate(
            flops=4 * kv_heads * rows * HD * (early + width),
            bytes_accessed=4 * prompt_k.size,
            transcendentals=kv_heads * rows * (early + width),
        ),
        name="attend",
    )(me, keys, values, bias, recv, *halves, *[pltpu.with_memory_space_constraint(x, pltpu.HBM) for x in far_early])
    back = lax.all_to_all(outputs, "branch", split_axis=0, concat_axis=0, tiled=True)
    return pl.pallas_call(
        post_kernel,
        out_shape=jax.ShapeDtypeStruct((row_count, q_width), jnp.bfloat16),
        in_specs=[SMEM, VMEM],
        out_specs=VMEM,
        scratch_shapes=[
            pltpu.SMEM((branches,), jnp.int32),
            pltpu.VMEM((row_count, heads, HD), jnp.float32),
        ],
        compiler_params=grant(8),
        name="post",
    )(owner_of, back)


def solution(mesh):
    split = ("groups", "branch")
    in_specs = (
        P(split, None, None),
        P(split, None, None),
        P(split, None),
        P(split, None, None),
        P(split),
        P(split, None),
        P(split, None),
        P(split, None),
        P(split, None),
    )
    return jax.shard_map(body, mesh=mesh, in_specs=in_specs, out_specs=P(split, None), check_vma=False)
```
